256 devices in a mesh: batch: 8 (over x_hi, y), patch: 32 (over x_lo, z, core).
Axes of the slice: x: 4 (x_hi: 2, x_lo: 2; x = x_hi * 2 + x_lo), y: 4, z: 8, core: 2. Of those that a mesh axis runs over, the one named last changes fastest.
Arguments:
- projections: bfloat16 [2, 3, 65536, 1536], P(None, None, ('batch', 'patch')), parts along dimension 2, may hold values from -6 to 6
- stale_cache: bfloat16 [2, 65536, 1536], P(None, ('batch', 'patch')), parts along dimension 1, may hold values from -8 to 8
- positions: int32 [3, 65536], P(None, ('batch', 'patch')), parts along dimension 1, may hold values from 0 to 63
- clip_lengths: int32 [128], P('batch'), parts along dimension 0, may hold values from 1 to 768, 8192 in all
- q_gain: float32 [1536], replicated, may hold values from 1.5 to 12
- k_gain: float32 [1536], replicated, may hold values from 1.5 to 12
Outputs:
- attended: bfloat16 [2, 65536, 1536], P(None, ('batch', 'patch')), parts along dimension 1
The draws below stay inside these ranges and needn't reach their ends.
There are 8 independent parts, one for each index of `batch`. The reference program is written for one: setup_inputs(seed, part) draws one part's arguments, and reference() takes and returns one part's arrays. A program takes and returns all parts, laid end to end along the dimension named above; an argument that names none is the same for every part. Nothing has to cross between parts.
Inputs may be any that keep to these rules, and one draw needn't show every extreme that they name: `clip_lengths`: clip lengths of one part sum to 8192; the longest is exactly 768 = 768, so a token's window holds its whole clip.
All inputs are finite; a program needn't handle non-finite values.
Results may differ from the reference program's by a relative error of at most 0.0017.
The reference program's roundings to bfloat16 on the way count: a program that leaves them out, or rounds other values in their place, can miss the bound.
Values may be sent and summed in bfloat16 or wider, within the bound.
No kernel may reach another device: no remote copies, remote signals or barrier semaphores. Data moves between devices by JAX's collectives and lax.ppermute only.
A program may use at most 128 MiB of HBM per device.

```python
import math
import jax
import jax.numpy as jnp
import numpy as np
from jax import lax

HEADS = 12
HEAD = 128
HD = 1536
TOK_DEV = 256
REACH = 3
STEPS = 2
MOST_CLIP = 768
TOKENS = 8192
NCLIP = 16
N_PATCH = 32


def channel_gains(key, head_top):
    first_key, second_key = jax.random.split(key)
    base = jnp.exp(jax.random.uniform(first_key, (HEADS, HEAD), jnp.float32, math.log(1.5), math.log(4.0)))
    factor = jnp.exp(jax.random.uniform(second_key, (HEADS, 1), jnp.float32, 0.0, math.log(head_top)))
    return (base * factor).reshape(HEADS * HEAD).astype(jnp.float32)


def draw_q_gain(key, part):
    key = jax.random.fold_in(key, 11)
    return channel_gains(key, 1.0)


def draw_k_gain(key, part):
    key = jax.random.fold_in(key, 23)
    return channel_gains(key, 1.0)


def place_ends(array, own_key, smallest, largest):
    shape = array.shape
    spot = [jax.random.randint(jax.random.fold_in(own_key, axis), (), 0, shape[axis]) for axis in range(len(shape))]
    array = array.at[tuple(spot)].set(smallest)
    longest = shape.index(max(shape))
    spot[longest] = (spot[longest] + 1) % shape[longest]
    return array.at[tuple(spot)].set(largest)


def level_of(own_key, shape, pieces, low, top_value):
    level = 1.0
    for position, shards_of in pieces:
        draws = jax.random.uniform(jax.random.fold_in(jax.random.fold_in(own_key, 6), position), (shards_of,), jnp.float32, low / len(pieces), top_value / len(pieces))
        level = level * jnp.repeat(jnp.exp(draws), shape[position] // shards_of).reshape((-1,) + (1,) * (len(shape) - 1 - position))
    return level


def split_up(amount, total, bound, skew):
    portions = [(1 << 20) // math.isqrt(grade ** skew) + 1 for grade in range(2, amount + 1)]
    surplus, given = total - bound - (amount - 1), [1] * (amount - 1)
    while surplus > 0:
        candidates = [i for i in range(amount - 1) if given[i] < bound]
        mass, remaining = sum([portions[i] for i in candidates]), surplus
        for i in candidates:
            extra = min(bound - given[i], max(1, remaining * portions[i] // mass), surplus)
            given[i] = given[i] + extra
            surplus = surplus - extra
    return np.array([bound] + given)


def ragged(key, count, total, reach, slope):
    if count == 2:
        one = jax.random.randint(key, (), max(1, total - reach), min(reach, total - 1) + 1)
        return jnp.stack([one, total - one])
    sizes = jnp.asarray(split_up(count, total, reach, slope), jnp.int32)
    pairs = (count - 1) // 2
    giver, sink = sizes[1:1 + 2 * pairs:2], sizes[2:2 + 2 * pairs:2]
    slack = jnp.minimum(giver - 1, reach - sink)
    moved = jax.random.randint(jax.random.fold_in(key, 1), (pairs,), 0, 1 << 20) % (slack + 1)
    sizes = sizes.at[1:1 + 2 * pairs:2].set(giver - moved).at[2:2 + 2 * pairs:2].set(sink + moved)
    return sizes[jax.random.permutation(jax.random.fold_in(key, 2), count)]


def bell_draw(rng, dims, width, bound, cuts=(), held_as=jnp.bfloat16):
    factor_of = level_of(rng, dims, cuts, -0.22, 0.18) if cuts else 1.0
    array = jax.random.normal(rng, dims, jnp.float32) * width * factor_of
    return jnp.minimum(jnp.maximum(array, -bound), bound).astype(held_as)


def setup_inputs(seed: int = 0, part: int = 0) -> dict:
    streams_of = jax.random.split(jax.random.key(seed), 7)
    part_splits = jax.random.split(jax.random.fold_in(streams_of[6], part), 7)
    return {
        "projections": bell_draw(part_splits[0], (STEPS, 3, TOKENS, HD), 1.0, 6.0, ((2, 32),)),
        "stale_cache": bell_draw(part_splits[1], (2, TOKENS, HD), 1.5, 8.0, ((1, 32),)),
        "positions": place_ends(jax.random.randint(part_splits[2], (3, TOKENS), 0, 64), jax.random.fold_in(part_splits[2], 1), 0, 63).astype(jnp.int32),
        "clip_lengths": ragged(part_splits[3], NCLIP, TOKENS, MOST_CLIP, 1).astype(jnp.int32),
        "q_gain": draw_q_gain(jax.random.fold_in(streams_of[6], 71), part),
        "k_gain": draw_k_gain(jax.random.fold_in(streams_of[6], 71), part),
    }


THETA = 256.0
NEG_FILL = -1e+30

def section_sizes(head_size):
    first_size = head_size // 8
    middle_size = (head_size - first_size) // 2
    return (first_size, middle_size, head_size - first_size - middle_size)

def rope_angles(positions, head_size):
    pieces_list = []
    for axis_number, section_width in enumerate(section_sizes(head_size)):
        halfway = section_width // 2
        exponent = -2.0 * jnp.arange(halfway, dtype=jnp.float32) / section_width
        frequency = jnp.power(jnp.float32(THETA), exponent)
        angles = positions[axis_number].astype(jnp.float32)[:, None] * frequency[None, :]
        pieces_list += [angles, angles]
    return jnp.concatenate(pieces_list, axis=1)

def rotation_table(head_size):
    table = np.zeros((head_size, head_size), np.float32)
    offset = 0
    for section_width in section_sizes(head_size):
        halfway = section_width // 2
        for column in range(halfway):
            table[offset + halfway + column, offset + column] = -1.0
            table[offset + column, offset + halfway + column] = 1.0
        offset += section_width
    return jnp.asarray(table, dtype=jnp.float32)

def norm_rope(raw, gain, cosines, sines, rotation, heads, head_size):
    row_count = raw.shape[0]
    values = raw.astype(jnp.float32).reshape(row_count, heads, head_size)
    inverse_rms = lax.rsqrt(lax.optimization_barrier(jnp.mean(values * values, axis=-1, keepdims=True)) + 1e-06)
    normed = values * inverse_rms * gain.reshape(heads, head_size)
    turned = jnp.einsum('nhd,de->nhe', normed, rotation, precision=lax.Precision.HIGHEST)
    rotated = normed * cosines[:, None, :] + turned * sines[:, None, :]
    return rotated.reshape(row_count, heads * head_size).astype(jnp.bfloat16)

def clip_of(index, clip_ends):
    return lax.optimization_barrier(jnp.sum((index[:, None] >= clip_ends[None, :]).astype(jnp.int32), axis=1))

def block_mask(block_number, tok_rows, clip_ends, token_count):
    query_index = block_number * tok_rows + jnp.arange(tok_rows, dtype=jnp.int32)
    key_index = (block_number - REACH) * tok_rows + jnp.arange((2 * REACH + 1) * tok_rows, dtype=jnp.int32)
    valid = (key_index >= 0) & (key_index < token_count)
    same_clip = clip_of(query_index, clip_ends)[:, None] == clip_of(key_index, clip_ends)[None, :]
    return same_clip & valid[None, :]

def attend(queries, keys, values, allowed, heads, head_size):
    row_count = queries.shape[0]
    key_count = keys.shape[0]
    head_queries = queries.astype(jnp.float32).reshape(row_count, heads, head_size)
    head_keys = keys.astype(jnp.float32).reshape(key_count, heads, head_size)
    head_values = values.astype(jnp.float32).reshape(key_count, heads, head_size)
    scores = jnp.einsum('qhd,khd->hqk', head_queries, head_keys) * (1.0 / math_sqrt(head_size))
    masked = jnp.where(allowed[None], scores, NEG_FILL)
    row_max = lax.optimization_barrier(jnp.max(masked, axis=2, keepdims=True))
    lifted = jnp.where(allowed[None], jnp.exp(masked - row_max), 0.0)
    weights = (lifted / lax.optimization_barrier(jnp.sum(lifted, axis=2, keepdims=True))).astype(jnp.bfloat16)
    mixed = jnp.einsum('hqk,khd->qhd', weights.astype(jnp.float32), head_values)
    return mixed.reshape(row_count, heads * head_size).astype(jnp.bfloat16)

def math_sqrt(number):
    return float(number) ** 0.5

def reference(projections, stale_cache, positions, clip_lengths, q_gain, k_gain):
    token_count = projections.shape[2]
    rotation = rotation_table(HEAD)
    angles = rope_angles(positions, HEAD)
    cosines = jnp.cos(angles)
    sines = jnp.sin(angles)
    clip_ends = jnp.cumsum(clip_lengths).astype(jnp.int32)
    window_rows = (2 * REACH + 1) * TOK_DEV
    carried = stale_cache
    results = []
    for step_index in range(STEPS):
        queries = norm_rope(projections[step_index, 0], q_gain, cosines, sines, rotation, HEADS, HEAD)
        keys = norm_rope(projections[step_index, 1], k_gain, cosines, sines, rotation, HEADS, HEAD)
        fresh = jnp.stack([keys, projections[step_index, 2]])
        padded = jnp.pad(carried, ((0, 0), (REACH * TOK_DEV, REACH * TOK_DEV), (0, 0)))

        def one_block(block_number, fresh=fresh, padded=padded, queries=queries):
            start = (block_number * TOK_DEV).astype(jnp.int32)
            window = lax.dynamic_slice_in_dim(padded, start, window_rows, axis=1)
            own_block = lax.dynamic_slice_in_dim(fresh, start, TOK_DEV, axis=1)
            window = jnp.concatenate([window[:, :REACH * TOK_DEV], own_block, window[:, (REACH + 1) * TOK_DEV:]], axis=1)
            block_queries = lax.dynamic_slice_in_dim(queries, start, TOK_DEV, axis=0)
            allowed = block_mask(block_number, TOK_DEV, clip_ends, token_count)
            return attend(block_queries, window[0], window[1], allowed, HEADS, HEAD)
        outputs = lax.map(one_block, jnp.arange(N_PATCH, dtype=jnp.int32))
        results.append(outputs.reshape(token_count, HEADS * HEAD))
        carried = fresh
    return jnp.stack(results)
```

```python
import functools

import jax
import jax.numpy as jnp
import numpy as np
from jax import lax
from jax.experimental import pallas as pl
from jax.experimental.pallas import tpu as pltpu
from jax.sharding import PartitionSpec as P

HEADS = 12
HEAD = 128
BLOCK = 256
HALF_HEADS = HEADS // 2
HALF = HALF_HEADS * HEAD
THETA = 256.0
SECTIONS = (16, 56, 56)
FAR = -(2.0**100)
LOG2E = 1.4426950408889634
SCORE_SCALE = LOG2E / float(HEAD) ** 0.5
ROLLS = (120, 8, 100, 28)


def rope_tables(positions):
    pieces = []
    for number, width in enumerate(SECTIONS):
        halfway = width // 2
        exponent = -2.0 * jnp.arange(halfway, dtype=jnp.float32) / width
        frequency = jnp.power(jnp.float32(THETA), exponent)
        angles = positions[number].astype(jnp.float32)[:, None] * frequency[None, :]
        pieces += [angles, angles]
    angles = jnp.concatenate(pieces, axis=1)
    sines = jnp.sin(angles)
    masks = np.zeros((4, HEAD), np.float32)
    masks[0, 0:8] = -1.0
    masks[1, 8:16] = 1.0
    masks[2, 16:44] = -1.0
    masks[2, 72:100] = -1.0
    masks[3, 44:72] = 1.0
    masks[3, 100:128] = 1.0
    return jnp.concatenate([jnp.cos(angles)[None], sines[None] * masks[:, None, :]], axis=0)


def prepare_kernel(core_ref, raw_ref, tables_ref, gains_ref, *out_refs):
    core = core_ref[0]
    q_outs, kv_outs = out_refs[:2], out_refs[2:]
    cosines = tables_ref[0]
    sines = [tables_ref[1 + i] for i in range(4)]
    for part in range(2):
        start = (core if part == 0 else 1 - core) * HALF
        for head in range(HALF_HEADS):
            columns = pl.ds(pl.multiple_of(start + head * HEAD, HEAD), HEAD)
            to = slice(head * HEAD, (head + 1) * HEAD)
            for kind in range(2):
                x = raw_ref[0, kind, :, columns].astype(jnp.float32)
                inverse = lax.rsqrt(jnp.mean(x * x, axis=-1, keepdims=True) + 1e-06)
                normed = x * inverse * gains_ref[kind : kind + 1, columns]
                rotated = normed * cosines
                for amount, sine in zip(ROLLS, sines):
                    rotated = rotated + pltpu.roll(normed, amount, 1) * sine
                rotated = rotated.astype(jnp.bfloat16)
                if kind == 0:
                    q_outs[part][:, to] = rotated
                else:
                    kv_outs[part][0, :, to] = rotated
            kv_outs[part][1, :, to] = raw_ref[0, 2, :, columns]


def prepare(core, projections, step, tables, gains):
    q_shape = jax.ShapeDtypeStruct((BLOCK, HALF), jnp.bfloat16)
    kv_shape = jax.ShapeDtypeStruct((2, BLOCK, HALF), jnp.bfloat16)
    return pl.pallas_call(
        prepare_kernel,
        grid=(1,),
        out_shape=(q_shape, q_shape, kv_shape, kv_shape),
        in_specs=[
            pl.BlockSpec(memory_space=pltpu.SMEM),
            pl.BlockSpec((1, 3, BLOCK, HEADS * HEAD), lambda i: (step, 0, 0, 0)),
            pl.BlockSpec((5, BLOCK, HEAD), lambda i: (0, 0, 0)),
            pl.BlockSpec((2, HEADS * HEAD), lambda i: (0, 0)),
        ],
        out_specs=(
            pl.BlockSpec((BLOCK, HALF), lambda i: (0, 0)),
            pl.BlockSpec((BLOCK, HALF), lambda i: (0, 0)),
            pl.BlockSpec((2, BLOCK, HALF), lambda i: (0, 0, 0)),
            pl.BlockSpec((2, BLOCK, HALF), lambda i: (0, 0, 0)),
        ),
        compiler_params=pltpu.CompilerParams(vmem_limit_bytes=24 * 2**20),
        cost_estimate=pl.CostEstimate(flops=20_000_000, bytes_accessed=6_000_000, transcendentals=0),
    )(core, projections, tables, gains)


def when(condition, body):
    if condition is True:
        body()
    else:
        pl.when(condition)(body)


def softmax_mix(blocks, query_of, key_of, value_of, scores, best, sums, out):
    heads = range(HALF_HEADS)
    first = blocks[0][0]
    for number, condition in blocks:

        def score(number=number):
            for h in heads:
                s = lax.dot_general(
                    query_of(h),
                    key_of(number, h),
                    (((1,), (1,)), ((), ())),
                    preferred_element_type=jnp.float32,
                )
                scores[number, h] = s
                m = jnp.maximum(s[:, :HEAD], s[:, HEAD:])
                best[h] = m if number == first else jnp.maximum(best[h], m)

        when(condition, score)
    for h in heads:
        top = jnp.max(best[h], axis=1, keepdims=True) * SCORE_SCALE
        best[h] = jnp.broadcast_to(top, (BLOCK, HEAD))
    for number, condition in blocks:

        def lift(number=number):
            for h in heads:
                top = best[h]
                low = jnp.exp2(scores[number, h, :, :HEAD] * SCORE_SCALE - top)
                high = jnp.exp2(scores[number, h, :, HEAD:] * SCORE_SCALE - top)
                scores[number, h, :, :HEAD] = low
                scores[number, h, :, HEAD:] = high
                sums[h] = low + high if number == first else sums[h] + (low + high)

        when(condition, lift)
    for h in heads:
        inverse = 1.0 / jnp.sum(sums[h], axis=1, keepdims=True)
        sums[h] = jnp.broadcast_to(inverse, (BLOCK, HEAD))
    for number, condition in blocks:

        def mix(number=number):
            for h in heads:
                inverse = sums[h]
                low = (scores[number, h, :, :HEAD] * inverse).astype(jnp.bfloat16)
                high = (scores[number, h, :, HEAD:] * inverse).astype(jnp.bfloat16)
                part = jnp.dot(
                    jnp.concatenate([low, high], axis=1),
                    value_of(number, h),
                    preferred_element_type=jnp.float32,
                )
                best[h] = part if number == first else best[h] + part

        when(condition, mix)
    for h in heads:
        out[:, columns(h)] = best[h].astype(jnp.bfloat16)


def columns(h):
    return slice(h * HEAD, (h + 1) * HEAD)


def own_kernel(split_last, switched, step, use_ref, qa_ref, ka_ref, q_ref, *rest):
    count = 8 + 2 * split_last + 2 * switched
    arrays, rest = rest[:count], rest[count:]
    outs, rest = rest[:2], rest[2:]
    q_buf, kv_buf, scores, best, sums, q_sem, kv_sem = rest
    fresh_low, fresh_high, old_low, old_high = arrays[:4]
    if split_last:
        l1, l2k, l2v, r1, r2k, r2v = arrays[4:10]
        l2, r2 = (l2k, l2v), (r2k, r2v)
    else:
        l1, l2, r1, r2 = arrays[4:8]
    queries = [pltpu.make_async_copy(q_ref.at[side, step], q_buf.at[side], q_sem.at[side]) for side in range(2)]
    for copy in queries:
        copy.start()

    def fetch(slot, source):
        if isinstance(source, tuple):
            for i in range(2):
                pltpu.make_async_copy(source[i], kv_buf.at[slot, i], kv_sem.at[slot, i]).start()
        else:
            for i in range(2):
                pltpu.make_async_copy(source.at[i], kv_buf.at[slot, i], kv_sem.at[slot, i]).start()

    def arrived(slot):
        for i in range(2):
            pltpu.make_async_copy(fresh_low.at[i], kv_buf.at[slot, i], kv_sem.at[slot, i]).wait()

    def needed(number):
        return use_ref[0, number] + use_ref[1, number] > 0

    fetch(0, fresh_low)
    cross_low = use_ref[0, 1] > 0
    pl.when(cross_low)(lambda: fetch(3, old_high))
    if switched:
        far = use_ref[2, 0] > 0
        near = jnp.logical_not(far)
        pl.when(jnp.logical_and(needed(2), near))(lambda: fetch(4, l1))
        pl.when(jnp.logical_and(needed(2), far))(lambda: fetch(4, arrays[count - 2]))
        pl.when(jnp.logical_and(needed(4), near))(lambda: fetch(6, r1))
        pl.when(jnp.logical_and(needed(4), far))(lambda: fetch(6, arrays[count - 1]))
    else:
        pl.when(needed(2))(lambda: fetch(4, l1))
        pl.when(needed(4))(lambda: fetch(6, r1))
    pl.when(needed(3))(lambda: fetch(5, l2))
    pl.when(needed(5))(lambda: fetch(7, r2))
    fetch(1, fresh_high)
    pl.when(use_ref[1, 0] > 0)(lambda: fetch(2, old_low))

    for side in range(2):
        queries[side].wait()
        if side == 0:
            arrived(0)
            pl.when(cross_low)(lambda: arrived(3))
            for number in range(2, 6):
                pl.when(needed(number))(lambda number=number: arrived(number + 2))
        else:
            arrived(1)
            pl.when(use_ref[1, 0] > 0)(lambda: arrived(2))

        def slot_of(number, side=side):
            if number >= 2:
                return number + 2
            return number if number == side else number + 2

        def query_of(h, side=side):
            return jnp.concatenate([q_buf[side, :, columns(h)], qa_ref[side]], axis=1)

        def key_of(number, h):
            return jnp.concatenate([kv_buf[slot_of(number), 0, :, columns(h)], ka_ref[number]], axis=1)

        def value_of(number, h):
            return kv_buf[slot_of(number), 1, :, columns(h)]

        blocks = [(side, True)] + [
            (n, use_ref[side, n] > 0) for n in [1 - side] + list(range(2, 6))
        ]
        softmax_mix(blocks, query_of, key_of, value_of, scores, best, sums, outs[side])


ANY = pl.BlockSpec(memory_space=pl.ANY)


def attend_own(step, use, qa, ka, queries, arrays, split_last, switched):
    shape = jax.ShapeDtypeStruct((BLOCK, HALF), jnp.bfloat16)
    whole = pl.BlockSpec((BLOCK, HALF), lambda i: (0, 0))
    return pl.pallas_call(
        functools.partial(own_kernel, split_last, switched, step),
        grid=(1,),
        out_shape=(shape, shape),
        in_specs=[
            pl.BlockSpec(memory_space=pltpu.SMEM),
            pl.BlockSpec((2, BLOCK, HEAD), lambda i: (0, 0, 0)),
            pl.BlockSpec((6, BLOCK, HEAD), lambda i: (0, 0, 0)),
            ANY,
        ]
        + [ANY] * len(arrays),
        out_specs=(whole, whole),
        scratch_shapes=[
            pltpu.VMEM((2, BLOCK, HALF), jnp.bfloat16),
            pltpu.VMEM((8, 2, BLOCK, HALF), jnp.bfloat16),
            pltpu.VMEM((6, HALF_HEADS, BLOCK, BLOCK), jnp.float32),
            pltpu.VMEM((HALF_HEADS, BLOCK, HEAD), jnp.float32),
            pltpu.VMEM((HALF_HEADS, BLOCK, HEAD), jnp.float32),
            pltpu.SemaphoreType.DMA((2,)),
            pltpu.SemaphoreType.DMA((8, 2)),
        ],
        compiler_params=pltpu.CompilerParams(vmem_limit_bytes=40 * 2**20),
        cost_estimate=pl.CostEstimate(
            flops=5_000_000_000, bytes_accessed=9_000_000, transcendentals=0
        ),
    )(use, qa, ka, queries, *arrays)


def far_kernel(step, fresh_split, far_ref, qa_ref, ka_ref, *rest):
    count = 8 + 2 * fresh_split
    arrays, rest = rest[:count], rest[count:]
    out, raw, packed, own, scores, best, sums, raw_sem, own_sem = rest
    q_left, q_right = arrays[0].at[step], arrays[1].at[step]
    if fresh_split:
        fresh = [(arrays[2], arrays[3]), (arrays[4], arrays[5])]
    else:
        fresh = [(a.at[0], a.at[1]) for a in arrays[2:4]]
    old_left, old_right, low, high = arrays[count - 4 :]
    sources = [
        (q_left, q_right),
        (fresh[0][0], fresh[1][0]),
        (fresh[0][1], fresh[1][1]),
        (old_left.at[0], old_right.at[0]),
        (old_left.at[1], old_right.at[1]),
    ]

    @pl.when(far_ref[0] > 0)
    def work():
        copies = []
        for i, pair in enumerate(sources):
            for j in range(2):
                copies.append(pltpu.make_async_copy(pair[j], raw.at[i, j], raw_sem.at[i, j]))
        for i, array in enumerate((low, high)):
            for j in range(2):
                copies.append(pltpu.make_async_copy(array.at[j], own.at[i, j], own_sem.at[i, j]))
        for copy in copies:
            copy.start()
        for copy in copies:
            copy.wait()
        from_right = lax.broadcasted_iota(jnp.int32, (BLOCK, HEAD), 0) < far_ref[1]
        for i in range(5):
            for h in range(HALF_HEADS):
                left = raw[i, 0, :, columns(h)].astype(jnp.float32)
                right = raw[i, 1, :, columns(h)].astype(jnp.float32)
                packed[i, :, columns(h)] = jnp.where(from_right, right, left).astype(jnp.bfloat16)

        def query_of(h):
            return jnp.concatenate([packed[0, :, columns(h)], qa_ref[...]], axis=1)

        def key_of(number, h):
            if number < 2:
                key = packed[1 + 2 * number, :, columns(h)]
            else:
                key = own[number - 2, 0, :, columns(h)]
            return jnp.concatenate([key, ka_ref[number]], axis=1)

        def value_of(number, h):
            if number < 2:
                return packed[2 + 2 * number, :, columns(h)]
            return own[number - 2, 1, :, columns(h)]

        softmax_mix(
            [(n, True) for n in range(4)], query_of, key_of, value_of, scores, best, sums, out
        )


def attend_far(step, far, qa, ka, arrays, fresh_split):
    return pl.pallas_call(
        functools.partial(far_kernel, step, fresh_split),
        grid=(1,),
        out_shape=jax.ShapeDtypeStruct((BLOCK, HALF), jnp.bfloat16),
        in_specs=[
            pl.BlockSpec(memory_space=pltpu.SMEM),
            pl.BlockSpec((BLOCK, HEAD), lambda i: (0, 0)),
            pl.BlockSpec((4, BLOCK, HEAD), lambda i: (0, 0, 0)),
        ]
        + [ANY] * len(arrays),
        out_specs=pl.BlockSpec((BLOCK, HALF), lambda i: (0, 0)),
        scratch_shapes=[
            pltpu.VMEM((5, 2, BLOCK, HALF), jnp.bfloat16),
            pltpu.VMEM((5, BLOCK, HALF), jnp.bfloat16),
            pltpu.VMEM((2, 2, BLOCK, HALF), jnp.bfloat16),
            pltpu.VMEM((4, HALF_HEADS, BLOCK, BLOCK), jnp.float32),
            pltpu.VMEM((HALF_HEADS, BLOCK, HEAD), jnp.float32),
            pltpu.VMEM((HALF_HEADS, BLOCK, HEAD), jnp.float32),
            pltpu.SemaphoreType.DMA((5, 2)),
            pltpu.SemaphoreType.DMA((2, 2)),
        ],
        compiler_params=pltpu.CompilerParams(vmem_limit_bytes=40 * 2**20),
        cost_estimate=pl.CostEstimate(
            flops=2_000_000_000, bytes_accessed=6_000_000, transcendentals=0
        ),
    )(far, qa, ka, *arrays)


def shards(projections, stale_cache, positions, clip_lengths, q_gain, k_gain):
    peers = lax.axis_size("patch")
    chips = peers // 2
    device = lax.axis_index("patch").astype(jnp.int32)
    core = device % 2
    chip = device // 2
    odd = core == 1

    def send(x, pairs):
        return lax.ppermute(x, "patch", pairs)

    def straight(by):
        return [(2 * c + t, 2 * (c + by) + t) for c in range(chips) for t in range(2) if 0 <= c + by < chips]

    def spread(to_right, to_other):
        pairs = []
        for c in range(chips):
            for t in range(2):
                there = c + (1 if t == to_right else -1)
                if 0 <= there < chips:
                    pairs.append((2 * c + t, 2 * there + (t ^ to_other)))
        return pairs

    def homeward(crossed):
        pairs = []
        for c in range(chips):
            for t in range(2):
                down = (t == 1) != crossed
                there = c + (-1 if down else 1)
                if 0 <= there < chips:
                    pairs.append((2 * c + t, 2 * there + (1 if down else 0)))
        return pairs

    swap_pairs = [(i, i ^ 1) for i in range(peers)]
    right, left = straight(1), straight(-1)

    def ordered(mine, peer):
        return jnp.where(odd, peer, mine), jnp.where(odd, mine, peer)

    stale_mine = lax.dynamic_slice_in_dim(stale_cache, core * HALF, HALF, axis=2)
    stale_other = lax.dynamic_slice_in_dim(stale_cache, (1 - core) * HALF, HALF, axis=2)
    first_a = send(stale_mine, spread(1, 0))
    first_b = send(stale_other, spread(1, 1))
    stale_peer = send(stale_other, swap_pairs)

    tables = rope_tables(positions)
    gains = jnp.stack([q_gain, k_gain])
    core_word = core[None]
    q0, q0_other, kv0, kv0_other = prepare(core_word, projections, 0, tables, gains)
    kv0_peer = send(kv0_other, swap_pairs)
    q1, q1_other, kv1, kv1_other = prepare(core_word, projections, 1, tables, gains)
    q_peer = send(jnp.stack([q0_other, q1_other]), swap_pairs)
    kv1_peer = send(kv1_other, swap_pairs)

    blocks = 2 * chip + jnp.array([0, 1, -1, -2, 2, 3], jnp.int32)
    ends = jnp.cumsum(clip_lengths).astype(jnp.int32)
    total = peers * BLOCK

    def clip_at(index):
        return jnp.sum((index[..., None] >= ends).astype(jnp.int32), axis=-1)

    index = blocks[:, None] * BLOCK + jnp.arange(BLOCK, dtype=jnp.int32)[None, :]
    clips = jnp.where(index < 0, -1, clip_at(index))
    starts = (chip + jnp.array([-1, 0, 1], jnp.int32)) * (2 * BLOCK)
    before, after = starts - 1, starts + 2 * BLOCK
    covered = (before >= 0) & (after < total) & (clip_at(before) == clip_at(after))
    far_below, far_here, far_above = covered[0], covered[1], covered[2]
    edge = jnp.min(jnp.where(ends > starts[1], ends, total)) - after[1]
    reach = starts[1] - jnp.max(jnp.where(ends <= starts[1], ends, 0))
    rows = jnp.arange(BLOCK, dtype=jnp.int32)
    side_right = rows < edge
    side_left = rows >= BLOCK - reach
    lane = jnp.arange(HEAD, dtype=jnp.int32)
    same = clips[:, :, None] == lane[None, None, :]
    ka = jnp.where(same, 0.0, 1.0).astype(jnp.bfloat16)
    qa = jnp.where(same[:2], FAR, 0.0).astype(jnp.bfloat16)
    of_left = side_left[:, None]
    of_right = side_right[:, None] & ~of_left
    left_lane, right_lane = lane[None, :] == 0, lane[None, :] == 1
    far_qa = jnp.where((of_left & left_lane) | (of_right & right_lane), FAR, 0.0).astype(jnp.bfloat16)
    barred_fresh = jnp.where(left_lane, ~of_left, ~of_right)
    barred_old = jnp.where(left_lane, ~of_right, ~of_left)
    none = jnp.zeros((BLOCK, HEAD), jnp.bool_)
    far_ka = jnp.stack([barred_fresh, barred_old, none, none]).astype(jnp.bfloat16)
    first, last = clips[:, 0], clips[:, -1]
    open_side = jnp.stack([~far_below, ~far_above])[jnp.array([0, 0, 1, 1])]
    open_block = jnp.concatenate([jnp.ones((2,), jnp.bool_), open_side])
    use = (
        (first[None, :] <= last[:2, None])
        & (last[None, :] >= first[:2, None])
        & (blocks >= 0)[None, :]
        & (blocks < peers)[None, :]
        & open_block[None, :]
    ).astype(jnp.int32)
    use = jnp.concatenate([use, jnp.broadcast_to(far_here.astype(jnp.int32), (1, 6))])
    far = jnp.stack([far_here.astype(jnp.int32), edge])
    gone_low = (far_below & (clips[0] == clip_at(starts[1] - 1)))[:, None]
    gone_high = (far_above & (clips[1] == clip_at(after[1])))[:, None]

    stale_low, stale_high = ordered(stale_mine, stale_peer)
    kv0_low, kv0_high = ordered(kv0, kv0_peer)
    q_low, q_high = ordered(jnp.stack([q0, q1]), q_peer)
    kv1_low, kv1_high = ordered(kv1, kv1_peer)
    queries = jnp.stack([q_low, q_high])

    second_l = send(jnp.where(far_above, kv0_high, stale_low), right)
    second_r = send(jnp.where(far_below, kv0_low, stale_high), left)
    third_l = send(jnp.where(far_above, q_high, kv0_high), right)
    third_r = send(jnp.where(far_below, q_low, kv0_low), left)
    first_r, first_l = ordered(first_a, first_b)
    fourth_l = send(jnp.where(far_above, kv1_high[0], kv0_low[0]), right)
    fourth_r = send(jnp.where(far_below, kv1_low[0], kv0_high[0]), left)

    own0 = attend_own(
        0, use, qa, ka, queries,
        (kv0_low, kv0_high, stale_low, stale_high, first_l, second_l, first_r, second_r),
        False, False,
    )
    far0 = attend_far(
        0, far, far_qa, far_ka,
        (third_l, third_r, second_l, second_r, first_l, first_r, stale_low, stale_high),
        False,
    )
    fifth_l = send(jnp.where(far_here, far0, jnp.where(far_above, kv1_high[1], kv0_low[1])), right)
    fifth_r = send(jnp.where(far_here, far0, jnp.where(far_below, kv1_low[1], kv0_high[1])), left)

    far1 = attend_far(
        1, far, far_qa, far_ka,
        (third_l, third_r, fourth_l, fifth_l, fourth_r, fifth_r, second_l, second_r, kv0_low, kv0_high),
        True,
    )
    home_mine = send(far1, homeward(False))
    home_other = send(far1, homeward(True))
    own1 = attend_own(
        1, use, qa, ka, queries,
        (kv1_low, kv1_high, kv0_low, kv0_high, third_l, fourth_l, fifth_l, third_r, fourth_r, fifth_r, second_l, second_r),
        True, True,
    )

    low0 = jnp.where(gone_low, fifth_l, own0[0])
    high0 = jnp.where(gone_high, fifth_r, own0[1])
    back0 = send(jnp.where(odd, low0, high0), swap_pairs)
    back1 = send(jnp.where(odd, own1[0], own1[1]), swap_pairs)
    gone = jnp.where(odd, gone_high, gone_low)
    mine0 = jnp.where(odd, high0, low0)
    mine1 = jnp.where(gone, home_mine, jnp.where(odd, own1[1], own1[0]))
    other1 = jnp.where(gone, home_other, back1)

    def whole(mine, other):
        return jnp.concatenate([jnp.where(odd, other, mine), jnp.where(odd, mine, other)], axis=1)

    return jnp.stack([whole(mine0, back0), whole(mine1, other1)])


def solution(mesh):
    return jax.shard_map(
        shards,
        mesh=mesh,
        in_specs=(
            P(None, None, ("batch", "patch"), None),
            P(None, ("batch", "patch"), None),
            P(None, ("batch", "patch")),
            P("batch"),
            P(),
            P(),
        ),
        out_specs=P(None, ("batch", "patch"), None),
        check_vma=False,
    )
```

```python
import functools

import jax
import jax.numpy as jnp
import numpy as np
from jax import lax
from jax.experimental import pallas as pl
from jax.experimental.pallas import tpu as pltpu
from jax.sharding import PartitionSpec as P

HEADS = 12
HEAD = 128
BLOCK = 256
HALF_HEADS = HEADS // 2
HALF = HALF_HEADS * HEAD
THETA = 256.0
SECTIONS = (16, 56, 56)
FAR = -(2.0**100)
LOG2E = 1.4426950408889634
SCORE_SCALE = LOG2E / float(HEAD) ** 0.5
FIRST_HALVES = ((0, 8), (16, 28), (72, 28))


def rope_tables(positions):
    section, frequency = [], []
    for number, width in enumerate(SECTIONS):
        halfway = width // 2
        exponent = -2.0 * jnp.arange(halfway, dtype=jnp.float32) / width
        one = jnp.power(jnp.float32(THETA), exponent)
        frequency += [one, one]
        section += [number] * width
    frequency = jnp.concatenate(frequency)[None, :]
    section = jnp.asarray(np.array(section, np.int32))[None, :]
    place = positions.astype(jnp.float32)[:, :, None]
    angles = jnp.where(section == 0, place[0], jnp.where(section == 1, place[1], place[2])) * frequency
    return jnp.stack([jnp.cos(angles), jnp.sin(angles)])


def partner_table():
    table = np.zeros((HEAD, HEAD), np.float32)
    for first, count in FIRST_HALVES:
        for e in range(first, first + count):
            table[e + count, e] = -1.0
            table[e, e + count] = 1.0
    return jnp.asarray(table, jnp.bfloat16)


def partners(gain):
    gain = gain.reshape(HEADS, HEAD)
    pieces = []
    for first, count in FIRST_HALVES:
        pieces += [gain[:, first + count : first + 2 * count], gain[:, first : first + count]]
    return jnp.concatenate(pieces, axis=1).reshape(HEADS * HEAD)


HBM = pl.BlockSpec(memory_space=pltpu.HBM)
VMEM = pl.BlockSpec(memory_space=pltpu.VMEM)
SMEM = pl.BlockSpec(memory_space=pltpu.SMEM)
CHEAP = pl.CostEstimate(flops=1, bytes_accessed=1, transcendentals=0)
ROOM = pltpu.CompilerParams(vmem_limit_bytes=60 * 2**20)


def columns(h):
    return slice(h * HEAD, (h + 1) * HEAD)


def when(condition, body):
    if condition is True:
        body()
    else:
        pl.when(condition)(body)


ODD, FAR_BELOW, FAR_HERE, FAR_ABOVE, EDGE, REACH, GONE_LOW, GONE_HIGH, FIRST = range(9)
USE = 9
WORDS = 21
BLOCK_STEPS = (0, 1, -1, -2, 2, 3)


def plan_kernel(device_ref, lengths_ref, plan_ref, bounds_ref):
    device = device_ref[0]
    base = (device // 2) * (2 * BLOCK)
    span = 2 * BLOCK
    clips = lengths_ref.shape[0]
    zero = jnp.int32(0)
    lane = lax.broadcasted_iota(jnp.int32, (8, HEAD), 1)
    low_bound = jnp.full((8, HEAD), 2**30, jnp.int32)
    high_bound = jnp.zeros((8, HEAD), jnp.int32)
    far = [zero, zero, zero]
    edge, reach, gone_low, gone_high = zero, zero, zero, jnp.int32(BLOCK)
    use = [[zero] * 6, [zero] * 6]
    start = zero
    for clip in range(clips):
        end = start + lengths_ref[clip]
        low_bound = jnp.where(lane == clip, start, low_bound)
        high_bound = jnp.where(lane == clip, end, high_bound)
        inside = []
        for step in BLOCK_STEPS:
            at = base + step * BLOCK
            inside.append(jnp.where((start < at + BLOCK) & (end > at), 1, 0))
        for side in range(2):
            use[side] = [u | (inside[side] & i) for u, i in zip(use[side], inside)]
        covers = []
        for by in (-1, 0, 1):
            at = base + by * span
            covers.append(jnp.where((start < at) & (end > at + span), 1, 0))
        far = [f | c for f, c in zip(far, covers)]
        edge = jnp.where(covers[1] > 0, end - base - span, edge)
        reach = jnp.where(covers[1] > 0, base - start, reach)
        gone_low = jnp.where(covers[0] > 0, end - base, gone_low)
        gone_high = jnp.where(covers[2] > 0, start - base - BLOCK, gone_high)
        start = end
    words = [device % 2] + far + [edge, reach, gone_low, gone_high, base]
    for side in range(2):
        words += use[side][:2]
        words += [u & (1 - far[0]) for u in use[side][2:4]]
        words += [u & (1 - far[2]) for u in use[side][4:6]]
    for place, word in enumerate(words):
        plan_ref[place] = word
    bounds_ref[0] = low_bound
    bounds_ref[1] = high_bound


def make_plan(device, clip_lengths):
    return pl.pallas_call(
        plan_kernel,
        out_shape=(
            jax.ShapeDtypeStruct((WORDS,), jnp.int32),
            jax.ShapeDtypeStruct((2, 8, HEAD), jnp.int32),
        ),
        in_specs=[SMEM, SMEM],
        out_specs=(SMEM, pl.BlockSpec(memory_space=pltpu.VMEM)),
        compiler_params=ROOM,
        cost_estimate=CHEAP,
    )(device, clip_lengths)


def one_hot(bounds_ref, first):
    token = first + lax.broadcasted_iota(jnp.int32, (BLOCK, HEAD), 0)
    return (token >= bounds_ref[0, :1, :]) & (token < bounds_ref[1, :1, :])


class Operands:
    def __init__(self):
        self.arrays = []

    def place(self, array):
        for at, held in enumerate(self.arrays):
            if held is array:
                return at
        self.arrays.append(array)
        return len(self.arrays) - 1

    def view(self, array, *lead, column=0, shared=False):
        return [(True, self.place(array), lead, column, shared)]

    def low(self, mine, peer):
        return [(0,) + mine[0][1:], (1,) + peer[0][1:]]

    def high(self, mine, peer):
        return [(1,) + mine[0][1:], (0,) + peer[0][1:]]


def copies_of(refs, view, width, target, sem, core):
    result = []
    for wanted, place, lead, column, shared in view:
        if shared:
            column = pl.multiple_of(core * HALF + column, HEAD)
        source = refs[place].at[lead + (slice(None), pl.ds(column, width))]
        result.append((wanted, functools.partial(pltpu.make_async_copy, source, target, sem)))
    return result


def start_copies(options, core, condition=True):
    for wanted, copy in options:
        parts = []
        if wanted is not True:
            parts.append(core == wanted)
        if condition is not True:
            parts.append(condition)
        begin = lambda copy=copy: copy().start()
        if not parts:
            begin()
        else:
            pl.when(functools.reduce(jnp.logical_and, parts))(begin)


def slice_kernel(core_ref, stale_ref, raw_ref, mine_ref, other_ref, swap_ref, buf, in_sem, out_sem):
    here = pl.multiple_of(core_ref[0] * HALF, HEAD)
    there = pl.multiple_of((1 - core_ref[0]) * HALF, HEAD)
    rows = []
    for i in range(2):
        rows.append((stale_ref.at[i, :, pl.ds(here, HALF)], [mine_ref.at[i]]))
        rows.append((stale_ref.at[i, :, pl.ds(there, HALF)], [other_ref.at[i], swap_ref.at[i]]))
    for i in range(2):
        rows.append((raw_ref.at[i, 2, :, pl.ds(there, HALF)], [swap_ref.at[2 + i]]))
    for i in range(2):
        for kind in range(2):
            rows.append((raw_ref.at[i, kind, :, pl.ds(there, HALF)], [swap_ref.at[4 + 2 * i + kind]]))
    through(rows, buf, in_sem, out_sem)


def through(rows, buf, in_sem, out_sem):
    loads = [
        pltpu.make_async_copy(source, buf.at[n], in_sem.at[n]) for n, (source, _) in enumerate(rows)
    ]
    for load in loads:
        load.start()
    stores = []
    for n, (_, targets) in enumerate(rows):
        loads[n].wait()
        for target in targets:
            store = pltpu.make_async_copy(buf.at[n], target, out_sem.at[len(stores)])
            store.start()
            stores.append(store)
    for store in stores:
        store.wait()


def slices(core, stale_cache, projections):
    def shape(n):
        return jax.ShapeDtypeStruct((n, BLOCK, HALF), jnp.bfloat16)

    return pl.pallas_call(
        slice_kernel,
        out_shape=(shape(2), shape(2), shape(8)),
        in_specs=[SMEM, HBM, HBM],
        out_specs=(HBM, HBM, HBM),
        scratch_shapes=[
            pltpu.VMEM((10, BLOCK, HALF), jnp.bfloat16),
            pltpu.SemaphoreType.DMA((10,)),
            pltpu.SemaphoreType.DMA((12,)),
        ],
        compiler_params=ROOM,
        cost_estimate=CHEAP,
    )(core, stale_cache, projections)


def prepare_kernel(core_ref, raw_ref, peer_ref, tables_ref, gains_ref, partner_ref, *outs):
    average = jnp.full((2 * HEAD, HEAD), 1.0 / HEAD, jnp.bfloat16)
    for part, raw in enumerate((raw_ref, peer_ref)):
        cosines, sines = tables_ref[part, 0], tables_ref[part, 1]
        for head in range(HALF_HEADS):
            for kind in range(2):
                row = raw[0, kind, :, columns(head)] if part == 0 else raw[kind, :, columns(head)]
                x = row.astype(jnp.float32)
                square = x * x
                high = square.astype(jnp.bfloat16)
                low = (square - high.astype(jnp.float32)).astype(jnp.bfloat16)
                mean = jnp.dot(
                    jnp.concatenate([high, low], axis=1), average, preferred_element_type=jnp.float32
                )
                other = jnp.dot(row, partner_ref[...], preferred_element_type=jnp.float32)
                inverse = lax.rsqrt(mean + 1e-06)
                normed = x * inverse * gains_ref[kind : kind + 1, columns(head)]
                turned = other * inverse * gains_ref[2 + kind : 3 + kind, columns(head)]
                rotated = normed * cosines + turned * sines
                outs[part][1 - kind, :, columns(head)] = rotated.astype(jnp.bfloat16)


def prepare(core, projections, raw_peer, tables, gains, partner):
    shape = jax.ShapeDtypeStruct((4, BLOCK, HALF), jnp.bfloat16)
    out = pl.BlockSpec((2, BLOCK, HALF), lambda i, core: (i, 0, 0))
    return pl.pallas_call(
        prepare_kernel,
        grid_spec=pltpu.PrefetchScalarGridSpec(
            num_scalar_prefetch=1,
            grid=(2,),
            in_specs=[
                pl.BlockSpec((1, 2, BLOCK, HALF), lambda i, core: (i, 0, 0, core[0])),
                pl.BlockSpec((2, BLOCK, HALF), lambda i, core: (2 + i, 0, 0)),
                pl.BlockSpec((2, 2, BLOCK, HEAD), lambda i, core: (0, 0, 0, 0)),
                pl.BlockSpec((4, HALF), lambda i, core: (0, core[0])),
                pl.BlockSpec((HEAD, HEAD), lambda i, core: (0, 0)),
            ],
            out_specs=(out, out),
        ),
        out_shape=(shape, shape),
        compiler_params=ROOM,
        cost_estimate=CHEAP,
    )(core, projections, raw_peer, tables, gains, partner)


def message_kernel(rows, count, plan_ref, *rest):
    refs, outs, (buf, in_sem, out_sem) = rest[:count], rest[count:-3], rest[-3:]
    core = plan_ref[ODD]
    loads, stores = [], []
    for number, (out, lead, width, choices) in enumerate(rows):
        target = buf.at[number, :, pl.ds(0, width)]
        for flag, value, view in choices:
            options = copies_of(refs, view, width, target, in_sem.at[number], core)
            condition = True if flag is None else plan_ref[flag] == value
            start_copies(options, core, condition)
        loads.append(options[0][1])
        stores.append(pltpu.make_async_copy(target, outs[out].at[lead], out_sem.at[number]))
    for load, store in zip(loads, stores):
        load().wait()
        store.start()
    for store in stores:
        store.wait()


def messages(plan, operands, outs, rows):
    return pl.pallas_call(
        functools.partial(message_kernel, rows, len(operands.arrays)),
        out_shape=tuple(jax.ShapeDtypeStruct(o, jnp.bfloat16) for o in outs),
        in_specs=[SMEM] + [HBM] * len(operands.arrays),
        out_specs=tuple(HBM for _ in outs),
        scratch_shapes=[
            pltpu.VMEM((len(rows), BLOCK, HALF), jnp.bfloat16),
            pltpu.SemaphoreType.DMA((len(rows),)),
            pltpu.SemaphoreType.DMA((len(rows),)),
        ],
        compiler_params=ROOM,
        cost_estimate=CHEAP,
    )(plan, *operands.arrays)


def softmax_mix(heads, blocks, query_of, key_of, value_of, scores, best, sums, out, ready=None):
    heads = range(heads)
    first = blocks[0][0]
    for number, condition in blocks:

        def score(number=number):
            if ready is not None:
                ready(number)
            for h in heads:
                s = lax.dot_general(
                    query_of(h),
                    key_of(number, h),
                    (((1,), (1,)), ((), ())),
                    preferred_element_type=jnp.float32,
                )
                scores[number, h] = s
                m = jnp.maximum(s[:, :HEAD], s[:, HEAD:])
                best[h] = m if number == first else jnp.maximum(best[h], m)

        when(condition, score)
    for h in heads:
        top = jnp.max(best[h], axis=1, keepdims=True) * SCORE_SCALE
        best[h] = jnp.broadcast_to(top, (BLOCK, HEAD))
    for number, condition in blocks:

        def lift(number=number):
            for h in heads:
                top = best[h]
                low = jnp.exp2(scores[number, h, :, :HEAD] * SCORE_SCALE - top)
                high = jnp.exp2(scores[number, h, :, HEAD:] * SCORE_SCALE - top)
                scores[number, h, :, :HEAD] = low
                scores[number, h, :, HEAD:] = high
                sums[h] = low + high if number == first else sums[h] + (low + high)

        when(condition, lift)
    for h in heads:
        inverse = 1.0 / jnp.sum(sums[h], axis=1, keepdims=True)
        sums[h] = jnp.broadcast_to(inverse, (BLOCK, HEAD))
    for number, condition in blocks:

        def mix(number=number):
            for h in heads:
                inverse = sums[h]
                low = (scores[number, h, :, :HEAD] * inverse).astype(jnp.bfloat16)
                high = (scores[number, h, :, HEAD:] * inverse).astype(jnp.bfloat16)
                part = jnp.dot(
                    jnp.concatenate([low, high], axis=1),
                    value_of(number, h),
                    preferred_element_type=jnp.float32,
                )
                best[h] = part if number == first else best[h] + part

        when(condition, mix)
    out(best)


def own_kernel(heads, queries, views, switched, plan_ref, bounds_ref, *rest):
    width = heads * HEAD
    refs, rest = rest[:-11], rest[-11:]
    outs, rest = rest[:2], rest[2:]
    q_buf, kv_buf, scores, best, sums, qa_ref, ka_ref, q_sem, kv_sem = rest
    core = plan_ref[ODD]

    def use(side, number):
        return plan_ref[USE + 6 * side + number] > 0

    def needed(number):
        return plan_ref[USE + number] + plan_ref[USE + 6 + number] > 0

    def options(slot, i, view):
        return copies_of(refs, view, width, kv_buf.at[slot, i], kv_sem.at[slot, i], core)

    def fetch(slot, condition=True, which=(0, 1)):
        for i in which:
            start_copies(options(slot, i, views[slot][i]), core, condition)

    def arrived(slot):
        for i in range(2):
            options(slot, i, views[slot][i])[0][1]().wait()

    query_options = [
        copies_of(refs, queries[side], width, q_buf.at[side], q_sem.at[side], core)
        for side in range(2)
    ]
    start_copies(query_options[0], core)
    fetch(0)
    fetch(3, use(0, 1))
    for number in range(2, 6):
        slot = number + 2
        if switched and slot in switched:
            far = plan_ref[FAR_HERE] > 0
            fetch(slot, needed(number), (0,))
            fetch(slot, jnp.logical_and(needed(number), jnp.logical_not(far)), (1,))
            start_copies(
                options(slot, 1, switched[slot]), core, jnp.logical_and(needed(number), far)
            )
        else:
            fetch(slot, needed(number))
    start_copies(query_options[1], core)
    fetch(1)
    fetch(2, use(1, 0))

    first = plan_ref[FIRST]
    for number, step in enumerate(BLOCK_STEPS):

        def mask(number=number, step=step):
            inside = one_hot(bounds_ref, first + step * BLOCK)
            ka_ref[number] = jnp.where(inside, 0.0, 1.0).astype(jnp.bfloat16)
            if number < 2:
                qa_ref[number] = jnp.where(inside, FAR, 0.0).astype(jnp.bfloat16)

        when(True if number < 2 else needed(number), mask)

    for side in range(2):
        query_options[side][0][1]().wait()

        def slot_of(number, side=side):
            if number >= 2:
                return number + 2
            return number if number == side else number + 2

        def ready(number, side=side):
            if side == 1 and number >= 2:
                pl.when(jnp.logical_not(use(0, number)))(lambda: arrived(slot_of(number)))
            else:
                arrived(slot_of(number))

        def query_of(h, side=side):
            return jnp.concatenate([q_buf[side, :, columns(h)], qa_ref[side]], axis=1)

        def key_of(number, h):
            return jnp.concatenate([kv_buf[slot_of(number), 0, :, columns(h)], ka_ref[number]], axis=1)

        def value_of(number, h):
            return kv_buf[slot_of(number), 1, :, columns(h)]

        def out(blocks, side=side):
            for place in range(2):

                @pl.when(core == (side + place) % 2)
                def store():
                    for h in range(heads):
                        outs[place][:, columns(h)] = blocks[h].astype(jnp.bfloat16)

        blocks = [(side, True)] + [(n, use(side, n)) for n in [1 - side] + list(range(2, 6))]
        softmax_mix(heads, blocks, query_of, key_of, value_of, scores, best, sums, out, ready)


def attend_own(heads, plan, bounds, operands, queries, views, switched=None):
    width = heads * HEAD
    shape = jax.ShapeDtypeStruct((BLOCK, width), jnp.bfloat16)
    whole = pl.BlockSpec((BLOCK, width), lambda i: (0, 0))
    return pl.pallas_call(
        functools.partial(own_kernel, heads, queries, views, switched),
        grid=(1,),
        out_shape=(shape, shape),
        in_specs=[SMEM, pl.BlockSpec((2, 8, HEAD), lambda i: (0, 0, 0))] + [HBM] * len(operands.arrays),
        out_specs=(whole, whole),
        scratch_shapes=[
            pltpu.VMEM((2, BLOCK, width), jnp.bfloat16),
            pltpu.VMEM((8, 2, BLOCK, width), jnp.bfloat16),
            pltpu.VMEM((6, heads, BLOCK, BLOCK), jnp.float32),
            pltpu.VMEM((heads, BLOCK, HEAD), jnp.float32),
            pltpu.VMEM((heads, BLOCK, HEAD), jnp.float32),
            pltpu.VMEM((2, BLOCK, HEAD), jnp.bfloat16),
            pltpu.VMEM((6, BLOCK, HEAD), jnp.bfloat16),
            pltpu.SemaphoreType.DMA((2,)),
            pltpu.SemaphoreType.DMA((8, 2)),
        ],
        compiler_params=ROOM,
        cost_estimate=CHEAP,
    )(plan, bounds, *operands.arrays)


def far_kernel(heads, pairs, own_views, before, plan_ref, *rest):
    width = heads * HEAD
    refs, rest = rest[:-10], rest[-10:]
    out_ref, raw, packed, own, scores, best, sums, qa_ref, ka_ref, sem = rest
    core = plan_ref[ODD]
    here = plan_ref[FAR_HERE] > 0

    @pl.when(here)
    def work():
        waits = []

        def load(view, target, number):
            halves = view if isinstance(view, tuple) else (view,)
            part = width // len(halves)
            for n, half in enumerate(halves):
                to = target.at[:, pl.ds(n * part, part)]
                options = copies_of(refs, half, part, to, sem.at[number, n], core)
                start_copies(options, core)
                waits.append(options[0][1])

        for i, pair in enumerate(pairs):
            for j in range(2):
                load(pair[j], raw.at[i, j], 2 * i + j)
        for i in range(2):
            for j in range(2):
                load(own_views[i][j], own.at[i, j], 10 + 2 * i + j)
        if before is not None:
            carried = functools.partial(
                pltpu.make_async_copy, refs[before], out_ref.at[0], sem.at[14, 0]
            )
            carried().start()
            waits.append(carried)
        row = lax.broadcasted_iota(jnp.int32, (BLOCK, HEAD), 0)
        lane = lax.broadcasted_iota(jnp.int32, (BLOCK, HEAD), 1)
        from_right = row < plan_ref[EDGE]
        of_left = jnp.where(row >= BLOCK - plan_ref[REACH], 1.0, 0.0)
        of_right = jnp.where(from_right, 1.0, 0.0)
        lefts = jnp.where(lane == 0, 1.0, 0.0)
        rights = jnp.where(lane == 1, 1.0, 0.0)
        qa_ref[...] = ((of_left * lefts + of_right * rights) * FAR).astype(jnp.bfloat16)
        ka_ref[0] = (lefts * (1.0 - of_left) + rights * (1.0 - of_right)).astype(jnp.bfloat16)
        ka_ref[1] = (lefts * (1.0 - of_right) + rights * (1.0 - of_left)).astype(jnp.bfloat16)
        ka_ref[2] = jnp.zeros((BLOCK, HEAD), jnp.bfloat16)
        for copy in waits:
            copy().wait()
        for i in range(5):
            for h in range(heads):
                left = raw[i, 0, :, columns(h)].astype(jnp.float32)
                right = raw[i, 1, :, columns(h)].astype(jnp.float32)
                packed[i, :, columns(h)] = jnp.where(from_right, right, left).astype(jnp.bfloat16)

        def query_of(h):
            return jnp.concatenate([packed[0, :, columns(h)], qa_ref[...]], axis=1)

        def key_of(number, h):
            if number < 2:
                key = packed[1 + 2 * number, :, columns(h)]
            else:
                key = own[number - 2, 0, :, columns(h)]
            return jnp.concatenate([key, ka_ref[min(number, 2)]], axis=1)

        def value_of(number, h):
            if number < 2:
                return packed[2 + 2 * number, :, columns(h)]
            return own[number - 2, 1, :, columns(h)]

        def out(blocks):
            for h in range(heads):
                at = (slice(None), columns(h)) if before is None else (1, slice(None), columns(h))
                out_ref[at] = blocks[h].astype(jnp.bfloat16)

        blocks = [(n, True) for n in range(4)]
        softmax_mix(heads, blocks, query_of, key_of, value_of, scores, best, sums, out)


def attend_far(heads, plan, operands, pairs, own_views, before=None):
    width = heads * HEAD
    shape = (BLOCK, width) if before is None else (2, BLOCK, width)
    return pl.pallas_call(
        functools.partial(far_kernel, heads, pairs, own_views, before),
        out_shape=jax.ShapeDtypeStruct(shape, jnp.bfloat16),
        in_specs=[SMEM] + [HBM] * len(operands.arrays),
        out_specs=pl.BlockSpec(shape, lambda: (0,) * len(shape)),
        scratch_shapes=[
            pltpu.VMEM((5, 2, BLOCK, width), jnp.bfloat16),
            pltpu.VMEM((5, BLOCK, width), jnp.bfloat16),
            pltpu.VMEM((2, 2, BLOCK, width), jnp.bfloat16),
            pltpu.VMEM((4, heads, BLOCK, BLOCK), jnp.float32),
            pltpu.VMEM((heads, BLOCK, HEAD), jnp.float32),
            pltpu.VMEM((heads, BLOCK, HEAD), jnp.float32),
            pltpu.VMEM((BLOCK, HEAD), jnp.bfloat16),
            pltpu.VMEM((3, BLOCK, HEAD), jnp.bfloat16),
            pltpu.SemaphoreType.DMA((15, 2)),
        ],
        compiler_params=ROOM,
        cost_estimate=CHEAP,
    )(plan, *operands.arrays)


def finish_kernel(plan_ref, *refs):
    keep0, back0, keep1, back1, home_mine, home_other, out_ref = refs
    core = plan_ref[ODD]
    row = lax.broadcasted_iota(jnp.int32, (BLOCK, HEAD), 0)
    low = jnp.where(core == 0, 0, plan_ref[GONE_HIGH])
    high = jnp.where(core == 0, plan_ref[GONE_LOW], BLOCK)
    gone = (row >= low) & (row < high)
    for half, (first, second, home) in enumerate(
        ((keep0, keep1, home_mine), (back0, back1, home_other))
    ):
        for h in range(HALF_HEADS):
            start = (core if half == 0 else 1 - core) * HALF + h * HEAD
            to = pl.ds(pl.multiple_of(start, HEAD), HEAD)
            rest = (first[:, columns(h)], second[:, columns(h)])
            for step in range(2):
                block = jnp.where(
                    gone, home[step, :, columns(h)].astype(jnp.float32), rest[step].astype(jnp.float32)
                )
                out_ref[step, :, to] = block.astype(jnp.bfloat16)


def finish(plan, *arrays):
    return pl.pallas_call(
        finish_kernel,
        out_shape=jax.ShapeDtypeStruct((2, BLOCK, HEADS * HEAD), jnp.bfloat16),
        in_specs=[SMEM] + [VMEM] * len(arrays),
        out_specs=VMEM,
        compiler_params=ROOM,
        cost_estimate=CHEAP,
    )(plan, *arrays)


def shards(projections, stale_cache, positions, clip_lengths, q_gain, k_gain):
    peers = lax.axis_size("patch")
    chips = peers // 2
    device = lax.axis_index("patch").astype(jnp.int32)
    core = device % 2
    odd = core == 1

    def send(x, pairs):
        return lax.ppermute(x, "patch", pairs)

    def straight(by):
        return [(2 * c + t, 2 * (c + by) + t) for c in range(chips) for t in range(2) if 0 <= c + by < chips]

    def spread(to_right, to_other):
        pairs = []
        for c in range(chips):
            for t in range(2):
                there = c + (1 if t == to_right else -1)
                if 0 <= there < chips:
                    pairs.append((2 * c + t, 2 * there + (t ^ to_other)))
        return pairs

    def homeward(crossed):
        pairs = []
        for c in range(chips):
            for t in range(2):
                down = (t == 1) != crossed
                there = c + (-1 if down else 1)
                if 0 <= there < chips:
                    pairs.append((2 * c + t, 2 * there + (1 if down else 0)))
        return pairs

    swap_pairs = [(i, i ^ 1) for i in range(peers)]
    right, left = straight(1), straight(-1)

    def after(value, *others):
        return lax.optimization_barrier((value,) + others)[0]

    core_word = core[None]
    wide = (2, BLOCK, HALF)

    stale_mine, stale_other, raw_other = slices(core_word, stale_cache, projections)
    first_a = send(stale_mine, spread(1, 0))
    first_b = send(stale_other, spread(1, 1))
    raw_peer = send(raw_other, swap_pairs)
    peer_positions = send(positions, swap_pairs)
    plan, bounds = make_plan(device[None], clip_lengths)

    class Views(Operands):
        def stale(self, which, i, column=0):
            return self.pick(which, self.view(stale_mine, i, column=column), self.view(raw_peer, i, column=column))

        def value(self, which, step, column=0):
            mine = self.view(projections, step, 2, column=column, shared=True)
            return self.pick(which, mine, self.view(raw_peer, 2 + step, column=column))

        def key(self, which, step, column=0):
            mine = self.view(kq, 2 * step, column=column)
            return self.pick(which, mine, self.view(kq_peer, 2 * step, column=column))

        def query(self, which, step, column=0):
            mine = self.view(kq, 2 * step + 1, column=column)
            return self.pick(which, mine, self.view(kq_peer, 2 * step + 1, column=column))

        def near(self, which, i):
            a, b = self.view(first_a, i), self.view(first_b, i)
            return [(1 - which,) + a[0][1:], (which,) + b[0][1:]]

        def pick(self, which, mine, peer):
            return self.high(mine, peer) if which else self.low(mine, peer)

        def both(self, array, column=0):
            return self.view(array, 0, column=column), self.view(array, 1, column=column)

    ops = Views()
    rows = []
    for out, flag in ((0, FAR_ABOVE), (1, FAR_BELOW)):
        for i in range(2):
            rows.append((out, i, HALF, [(flag, 0, ops.stale(out, i)), (flag, 1, ops.value(1 - out, i))]))
    message_l, message_r = messages(plan, ops, (wide, wide), rows)
    second_l = send(message_l, right)
    second_r = send(message_r, left)

    tables = jnp.stack([rope_tables(positions), rope_tables(peer_positions)])
    gains = jnp.stack([q_gain, k_gain, partners(q_gain), partners(k_gain)])
    kq, kq_peer = prepare(after(core_word, message_l), projections, raw_peer, tables, gains, partner_table())

    ops = Views()
    rows = []
    for out, flag in ((0, FAR_ABOVE), (1, FAR_BELOW)):
        near = 1 - out
        rows.append((out, 0, HALF, [(None, 0, ops.key(near, 0))]))
        rows.append((out, 1, HALF, [(flag, 0, ops.value(near, 0)), (flag, 1, ops.query(near, 0))]))
        rows.append((2 + out, 0, HALF, [(flag, 0, ops.key(out, 0)), (flag, 1, ops.query(near, 1))]))
        rows.append((2 + out, 1, HALF, [(flag, 0, ops.value(out, 0)), (flag, 1, ops.key(near, 1))]))
    third_out_l, third_out_r, fourth_out_l, fourth_out_r = messages(
        after(plan, first_a, first_b), ops, (wide,) * 4, rows
    )
    third_l = send(third_out_l, right)
    third_r = send(third_out_r, left)

    fourth_l = send(fourth_out_l, right)
    fourth_r = send(fourth_out_r, left)

    ops = Views()
    keep0, give0 = attend_own(
        HALF_HEADS, after(plan, third_out_l), bounds, ops,
        [ops.query(0, 0), ops.query(1, 0)],
        [
            (ops.key(0, 0), ops.value(0, 0)),
            (ops.key(1, 0), ops.value(1, 0)),
            (ops.stale(0, 0), ops.stale(0, 1)),
            (ops.stale(1, 0), ops.stale(1, 1)),
            (ops.near(0, 0), ops.near(0, 1)),
            ops.both(second_l),
            (ops.near(1, 0), ops.near(1, 1)),
            ops.both(second_r),
        ],
    )
    back0 = send(give0, swap_pairs)

    def far_step(step, plan, query_key, before=None):
        ops = Views()
        if step == 0:
            old = [(ops.near(0, i), ops.near(1, i)) for i in range(2)]
            own = [(ops.stale(i, 0), ops.stale(i, 1)) for i in range(2)]
        else:
            old = [
                (ops.view(third_l, 0), ops.view(third_r, 0)),
                (ops.view(second_l, 0), ops.view(second_r, 0)),
            ]
            own = [(ops.key(i, 0), ops.value(i, 0)) for i in range(2)]
        pairs = [tuple(query_key(ops, side, i) for side in range(2)) for i in range(2)]
        pairs += [(ops.view(second_l, step), ops.view(second_r, step))] + old
        place = None if before is None else ops.place(before)
        return attend_far(HALF_HEADS, plan, ops, pairs, own, place)

    far0 = far_step(0, after(plan, give0), lambda ops, side, i: ops.view((third_l, third_r)[side], 1 - i))
    far1 = far_step(
        1, after(plan, back0), lambda ops, side, i: ops.view((fourth_l, fourth_r)[side], i), far0
    )
    home_mine = send(far1, homeward(False))
    home_other = send(far1, homeward(True))
    ops = Views()
    keep1, give1 = attend_own(
        HALF_HEADS, after(plan, far1), bounds, ops,
        [ops.query(0, 1), ops.query(1, 1)],
        [
            (ops.key(0, 1), ops.value(0, 1)),
            (ops.key(1, 1), ops.value(1, 1)),
            (ops.key(0, 0), ops.value(0, 0)),
            (ops.key(1, 0), ops.value(1, 0)),
            ops.both(third_l),
            ops.both(fourth_l),
            ops.both(third_r),
            ops.both(fourth_r),
        ],
        {4: ops.view(second_l, 0), 6: ops.view(second_r, 0)},
    )
    back1 = send(give1, swap_pairs)
    return finish(plan, keep0, back0, keep1, back1, home_mine, home_other)


def solution(mesh):
    return jax.shard_map(
        shards,
        mesh=mesh,
        in_specs=(
            P(None, None, ("batch", "patch"), None),
            P(None, ("batch", "patch"), None),
            P(None, ("batch", "patch")),
            P("batch"),
            P(),
            P(),
        ),
        out_specs=P(None, ("batch", "patch"), None),
        check_vma=False,
    )
```

```python
import functools

import jax
import jax.numpy as jnp
import numpy as np
from jax import lax
from jax.experimental import pallas as pl
from jax.experimental.pallas import tpu as pltpu
from jax.sharding import PartitionSpec as P

HEADS = 12
HEAD = 128
BLOCK = 256
HALF_HEADS = HEADS // 2
HALF = HALF_HEADS * HEAD
THETA = 256.0
SECTIONS = (16, 56, 56)
FAR = -(2.0**100)
LOG2E = 1.4426950408889634
SCORE_SCALE = LOG2E / float(HEAD) ** 0.5
FIRST_HALVES = ((0, 8), (16, 28), (72, 28))


def rope_tables(positions):
    section, frequency = [], []
    for number, width in enumerate(SECTIONS):
        halfway = width // 2
        exponent = -2.0 * jnp.arange(halfway, dtype=jnp.float32) / width
        one = jnp.power(jnp.float32(THETA), exponent)
        frequency += [one, one]
        section += [number] * width
    frequency = jnp.concatenate(frequency)[None, :]
    section = jnp.asarray(np.array(section, np.int32))[None, :]
    place = positions.astype(jnp.float32)[:, :, None]
    angles = jnp.where(section == 0, place[0], jnp.where(section == 1, place[1], place[2])) * frequency
    return jnp.stack([jnp.cos(angles), jnp.sin(angles)])


def partner_table():
    table = np.zeros((HEAD, HEAD), np.float32)
    for first, count in FIRST_HALVES:
        for e in range(first, first + count):
            table[e + count, e] = -1.0
            table[e, e + count] = 1.0
    return jnp.asarray(table, jnp.bfloat16)


def partners(gain):
    gain = gain.reshape(HEADS, HEAD)
    pieces = []
    for first, count in FIRST_HALVES:
        pieces += [gain[:, first + count : first + 2 * count], gain[:, first : first + count]]
    return jnp.concatenate(pieces, axis=1).reshape(HEADS * HEAD)


HBM = pl.BlockSpec(memory_space=pltpu.HBM)
VMEM = pl.BlockSpec(memory_space=pltpu.VMEM)
SMEM = pl.BlockSpec(memory_space=pltpu.SMEM)
CHEAP = pl.CostEstimate(flops=1, bytes_accessed=1, transcendentals=0)
ROOM = pltpu.CompilerParams(vmem_limit_bytes=60 * 2**20)


def columns(h):
    return slice(h * HEAD, (h + 1) * HEAD)


def when(condition, body):
    if condition is True:
        body()
    else:
        pl.when(condition)(body)


ODD, FAR_BELOW, FAR_HERE, FAR_ABOVE, EDGE, REACH, GONE_LOW, GONE_HIGH, FIRST = range(9)
USE = 9
WORDS = 21
BLOCK_STEPS = (0, 1, -1, -2, 2, 3)


def plan_kernel(device_ref, lengths_ref, plan_ref, bounds_ref):
    device = device_ref[0]
    base = (device // 2) * (2 * BLOCK)
    span = 2 * BLOCK
    clips = lengths_ref.shape[0]
    zero = jnp.int32(0)
    lane = lax.broadcasted_iota(jnp.int32, (8, HEAD), 1)
    low_bound = jnp.full((8, HEAD), 2**30, jnp.int32)
    high_bound = jnp.zeros((8, HEAD), jnp.int32)
    far = [zero, zero, zero]
    edge, reach, gone_low, gone_high = zero, zero, zero, jnp.int32(BLOCK)
    use = [[zero] * 6, [zero] * 6]
    start = zero
    for clip in range(clips):
        end = start + lengths_ref[clip]
        low_bound = jnp.where(lane == clip, start, low_bound)
        high_bound = jnp.where(lane == clip, end, high_bound)
        inside = []
        for step in BLOCK_STEPS:
            at = base + step * BLOCK
            inside.append(jnp.where((start < at + BLOCK) & (end > at), 1, 0))
        for side in range(2):
            use[side] = [u | (inside[side] & i) for u, i in zip(use[side], inside)]
        covers = []
        for by in (-1, 0, 1):
            at = base + by * span
            covers.append(jnp.where((start < at) & (end > at + span), 1, 0))
        far = [f | c for f, c in zip(far, covers)]
        edge = jnp.where(covers[1] > 0, end - base - span, edge)
        reach = jnp.where(covers[1] > 0, base - start, reach)
        gone_low = jnp.where(covers[0] > 0, end - base, gone_low)
        gone_high = jnp.where(covers[2] > 0, start - base - BLOCK, gone_high)
        start = end
    words = [device % 2] + far + [edge, reach, gone_low, gone_high, base]
    for side in range(2):
        words += use[side][:2]
        words += [u & (1 - far[0]) for u in use[side][2:4]]
        words += [u & (1 - far[2]) for u in use[side][4:6]]
    for place, word in enumerate(words):
        plan_ref[place] = word
    bounds_ref[0] = low_bound
    bounds_ref[1] = high_bound


def make_plan(device, clip_lengths):
    return pl.pallas_call(
        plan_kernel,
        out_shape=(
            jax.ShapeDtypeStruct((WORDS,), jnp.int32),
            jax.ShapeDtypeStruct((2, 8, HEAD), jnp.int32),
        ),
        in_specs=[SMEM, SMEM],
        out_specs=(SMEM, pl.BlockSpec(memory_space=pltpu.VMEM)),
        compiler_params=ROOM,
        cost_estimate=CHEAP,
    )(device, clip_lengths)


def one_hot(bounds_ref, first):
    token = first + lax.broadcasted_iota(jnp.int32, (BLOCK, HEAD), 0)
    return (token >= bounds_ref[0, :1, :]) & (token < bounds_ref[1, :1, :])


class Operands:
    def __init__(self):
        self.arrays = []

    def place(self, array):
        for at, held in enumerate(self.arrays):
            if held is array:
                return at
        self.arrays.append(array)
        return len(self.arrays) - 1

    def view(self, array, *lead, column=0, shared=False):
        return [(True, self.place(array), lead, column, shared)]

    def low(self, mine, peer):
        return [(0,) + mine[0][1:], (1,) + peer[0][1:]]

    def high(self, mine, peer):
        return [(1,) + mine[0][1:], (0,) + peer[0][1:]]


def copies_of(refs, view, width, target, sem, core):
    result = []
    for wanted, place, lead, column, shared in view:
        if shared:
            column = pl.multiple_of(core * HALF + column, HEAD)
        source = refs[place].at[lead + (slice(None), pl.ds(column, width))]
        result.append((wanted, functools.partial(pltpu.make_async_copy, source, target, sem)))
    return result


def start_copies(options, core, condition=True):
    for wanted, copy in options:
        parts = []
        if wanted is not True:
            parts.append(core == wanted)
        if condition is not True:
            parts.append(condition)
        begin = lambda copy=copy: copy().start()
        if not parts:
            begin()
        else:
            pl.when(functools.reduce(jnp.logical_and, parts))(begin)


def slice_kernel(core_ref, stale_ref, raw_ref, mine_ref, other_ref, swap_ref, buf, in_sem, out_sem):
    here = pl.multiple_of(core_ref[0] * HALF, HEAD)
    there = pl.multiple_of((1 - core_ref[0]) * HALF, HEAD)
    rows = []
    for i in range(2):
        rows.append((stale_ref.at[i, :, pl.ds(here, HALF)], [mine_ref.at[i]]))
        rows.append((stale_ref.at[i, :, pl.ds(there, HALF)], [other_ref.at[i], swap_ref.at[i]]))
    for i in range(2):
        rows.append((raw_ref.at[i, 2, :, pl.ds(there, HALF)], [swap_ref.at[2 + i]]))
    for i in range(2):
        for kind in range(2):
            rows.append((raw_ref.at[i, kind, :, pl.ds(there, HALF)], [swap_ref.at[4 + 2 * i + kind]]))
    through(rows, buf, in_sem, out_sem)


def through(rows, buf, in_sem, out_sem):
    loads = [
        pltpu.make_async_copy(source, buf.at[n], in_sem.at[n]) for n, (source, _) in enumerate(rows)
    ]
    for load in loads:
        load.start()
    stores = []
    for n, (_, targets) in enumerate(rows):
        loads[n].wait()
        for target in targets:
            store = pltpu.make_async_copy(buf.at[n], target, out_sem.at[len(stores)])
            store.start()
            stores.append(store)
    for store in stores:
        store.wait()


def slices(core, stale_cache, projections):
    def shape(n):
        return jax.ShapeDtypeStruct((n, BLOCK, HALF), jnp.bfloat16)

    return pl.pallas_call(
        slice_kernel,
        out_shape=(shape(2), shape(2), shape(8)),
        in_specs=[SMEM, HBM, HBM],
        out_specs=(HBM, HBM, HBM),
        scratch_shapes=[
            pltpu.VMEM((10, BLOCK, HALF), jnp.bfloat16),
            pltpu.SemaphoreType.DMA((10,)),
            pltpu.SemaphoreType.DMA((12,)),
        ],
        compiler_params=ROOM,
        cost_estimate=CHEAP,
    )(core, stale_cache, projections)


def prepare_kernel(core_ref, raw_ref, peer_ref, tables_ref, gains_ref, partner_ref, *outs):
    average = jnp.full((2 * HEAD, HEAD), 1.0 / HEAD, jnp.bfloat16)
    for part, raw in enumerate((raw_ref, peer_ref)):
        cosines, sines = tables_ref[part, 0], tables_ref[part, 1]
        for head in range(HALF_HEADS):
            for kind in range(2):
                row = raw[0, kind, :, columns(head)] if part == 0 else raw[kind, :, columns(head)]
                x = row.astype(jnp.float32)
                square = x * x
                high = square.astype(jnp.bfloat16)
                low = (square - high.astype(jnp.float32)).astype(jnp.bfloat16)
                mean = jnp.dot(
                    jnp.concatenate([high, low], axis=1), average, preferred_element_type=jnp.float32
                )
                other = jnp.dot(row, partner_ref[...], preferred_element_type=jnp.float32)
                inverse = lax.rsqrt(mean + 1e-06)
                normed = x * inverse * gains_ref[kind : kind + 1, columns(head)]
                turned = other * inverse * gains_ref[2 + kind : 3 + kind, columns(head)]
                rotated = normed * cosines + turned * sines
                outs[part][1 - kind, :, columns(head)] = rotated.astype(jnp.bfloat16)


def prepare(core, projections, raw_peer, tables, gains, partner):
    shape = jax.ShapeDtypeStruct((4, BLOCK, HALF), jnp.bfloat16)
    out = pl.BlockSpec((2, BLOCK, HALF), lambda i, core: (i, 0, 0))
    return pl.pallas_call(
        prepare_kernel,
        grid_spec=pltpu.PrefetchScalarGridSpec(
            num_scalar_prefetch=1,
            grid=(2,),
            in_specs=[
                pl.BlockSpec((1, 2, BLOCK, HALF), lambda i, core: (i, 0, 0, core[0])),
                pl.BlockSpec((2, BLOCK, HALF), lambda i, core: (2 + i, 0, 0)),
                pl.BlockSpec((2, 2, BLOCK, HEAD), lambda i, core: (0, 0, 0, 0)),
                pl.BlockSpec((4, HALF), lambda i, core: (0, core[0])),
                pl.BlockSpec((HEAD, HEAD), lambda i, core: (0, 0)),
            ],
            out_specs=(out, out),
        ),
        out_shape=(shape, shape),
        compiler_params=ROOM,
        cost_estimate=CHEAP,
    )(core, projections, raw_peer, tables, gains, partner)


def message_kernel(rows, count, plan_ref, *rest):
    refs, outs, (buf, in_sem, out_sem) = rest[:count], rest[count:-3], rest[-3:]
    core = plan_ref[ODD]
    loads, stores = [], []
    for number, (out, lead, width, choices) in enumerate(rows):
        target = buf.at[number, :, pl.ds(0, width)]
        for flag, value, view in choices:
            options = copies_of(refs, view, width, target, in_sem.at[number], core)
            condition = True if flag is None else plan_ref[flag] == value
            start_copies(options, core, condition)
        loads.append(options[0][1])
        stores.append(pltpu.make_async_copy(target, outs[out].at[lead], out_sem.at[number]))
    for load, store in zip(loads, stores):
        load().wait()
        store.start()
    for store in stores:
        store.wait()


def messages(plan, operands, outs, rows):
    return pl.pallas_call(
        functools.partial(message_kernel, rows, len(operands.arrays)),
        out_shape=tuple(jax.ShapeDtypeStruct(o, jnp.bfloat16) for o in outs),
        in_specs=[SMEM] + [HBM] * len(operands.arrays),
        out_specs=tuple(HBM for _ in outs),
        scratch_shapes=[
            pltpu.VMEM((len(rows), BLOCK, HALF), jnp.bfloat16),
            pltpu.SemaphoreType.DMA((len(rows),)),
            pltpu.SemaphoreType.DMA((len(rows),)),
        ],
        compiler_params=ROOM,
        cost_estimate=CHEAP,
    )(plan, *operands.arrays)


def softmax_mix(heads, blocks, query_of, key_of, value_of, scores, best, sums, out, ready=None):
    heads = range(heads)
    first = blocks[0][0]
    for number, condition in blocks:

        def score(number=number):
            if ready is not None:
                ready(number)
            for h in heads:
                s = lax.dot_general(
                    query_of(h),
                    key_of(number, h),
                    (((1,), (1,)), ((), ())),
                    preferred_element_type=jnp.float32,
                )
                scores[number, h] = s
                m = jnp.maximum(s[:, :HEAD], s[:, HEAD:])
                best[h] = m if number == first else jnp.maximum(best[h], m)

        when(condition, score)
    for h in heads:
        top = jnp.max(best[h], axis=1, keepdims=True) * SCORE_SCALE
        best[h] = jnp.broadcast_to(top, (BLOCK, HEAD))
    for number, condition in blocks:

        def lift(number=number):
            for h in heads:
                top = best[h]
                low = jnp.exp2(scores[number, h, :, :HEAD] * SCORE_SCALE - top)
                high = jnp.exp2(scores[number, h, :, HEAD:] * SCORE_SCALE - top)
                scores[number, h, :, :HEAD] = low
                scores[number, h, :, HEAD:] = high
                sums[h] = low + high if number == first else sums[h] + (low + high)

        when(condition, lift)
    for h in heads:
        inverse = 1.0 / jnp.sum(sums[h], axis=1, keepdims=True)
        sums[h] = jnp.broadcast_to(inverse, (BLOCK, HEAD))
    for number, condition in blocks:

        def mix(number=number):
            for h in heads:
                inverse = sums[h]
                low = (scores[number, h, :, :HEAD] * inverse).astype(jnp.bfloat16)
                high = (scores[number, h, :, HEAD:] * inverse).astype(jnp.bfloat16)
                part = jnp.dot(
                    jnp.concatenate([low, high], axis=1),
                    value_of(number, h),
                    preferred_element_type=jnp.float32,
                )
                best[h] = part if number == first else best[h] + part

        when(condition, mix)
    out(best)


def own_kernel(heads, queries, views, switched, plan_ref, bounds_ref, *rest):
    width = heads * HEAD
    refs, rest = rest[:-11], rest[-11:]
    outs, rest = rest[:2], rest[2:]
    q_buf, kv_buf, scores, best, sums, qa_ref, ka_ref, q_sem, kv_sem = rest
    core = plan_ref[ODD]

    def use(side, number):
        return plan_ref[USE + 6 * side + number] > 0

    def needed(number):
        return plan_ref[USE + number] + plan_ref[USE + 6 + number] > 0

    def options(slot, i, view):
        return copies_of(refs, view, width, kv_buf.at[slot, i], kv_sem.at[slot, i], core)

    def fetch(slot, condition=True, which=(0, 1)):
        for i in which:
            start_copies(options(slot, i, views[slot][i]), core, condition)

    def arrived(slot):
        for i in range(2):
            options(slot, i, views[slot][i])[0][1]().wait()

    query_options = [
        copies_of(refs, queries[side], width, q_buf.at[side], q_sem.at[side], core)
        for side in range(2)
    ]
    start_copies(query_options[0], core)
    fetch(0)
    fetch(3, use(0, 1))
    for number in range(2, 6):
        slot = number + 2
        if switched and slot in switched:
            far = plan_ref[FAR_HERE] > 0
            fetch(slot, needed(number), (0,))
            fetch(slot, jnp.logical_and(needed(number), jnp.logical_not(far)), (1,))
            start_copies(
                options(slot, 1, switched[slot]), core, jnp.logical_and(needed(number), far)
            )
        else:
            fetch(slot, needed(number))
    start_copies(query_options[1], core)
    fetch(1)
    fetch(2, use(1, 0))

    first = plan_ref[FIRST]
    for number, step in enumerate(BLOCK_STEPS):

        def mask(number=number, step=step):
            inside = one_hot(bounds_ref, first + step * BLOCK)
            ka_ref[number] = jnp.where(inside, 0.0, 1.0).astype(jnp.bfloat16)
            if number < 2:
                qa_ref[number] = jnp.where(inside, FAR, 0.0).astype(jnp.bfloat16)

        when(True if number < 2 else needed(number), mask)

    for side in range(2):
        query_options[side][0][1]().wait()

        def slot_of(number, side=side):
            if number >= 2:
                return number + 2
            return number if number == side else number + 2

        def ready(number, side=side):
            if side == 1 and number >= 2:
                pl.when(jnp.logical_not(use(0, number)))(lambda: arrived(slot_of(number)))
            else:
                arrived(slot_of(number))

        def query_of(h, side=side):
            return jnp.concatenate([q_buf[side, :, columns(h)], qa_ref[side]], axis=1)

        def key_of(number, h):
            return jnp.concatenate([kv_buf[slot_of(number), 0, :, columns(h)], ka_ref[number]], axis=1)

        def value_of(number, h):
            return kv_buf[slot_of(number), 1, :, columns(h)]

        def out(blocks, side=side):
            for place in range(2):

                @pl.when(core == (side + place) % 2)
                def store():
                    for h in range(heads):
                        outs[place][:, columns(h)] = blocks[h].astype(jnp.bfloat16)

        blocks = [(side, True)] + [(n, use(side, n)) for n in [1 - side] + list(range(2, 6))]
        softmax_mix(heads, blocks, query_of, key_of, value_of, scores, best, sums, out, ready)


def attend_own(heads, plan, bounds, operands, queries, views, switched=None):
    width = heads * HEAD
    shape = jax.ShapeDtypeStruct((BLOCK, width), jnp.bfloat16)
    whole = pl.BlockSpec((BLOCK, width), lambda i: (0, 0))
    return pl.pallas_call(
        functools.partial(own_kernel, heads, queries, views, switched),
        grid=(1,),
        out_shape=(shape, shape),
        in_specs=[SMEM, pl.BlockSpec((2, 8, HEAD), lambda i: (0, 0, 0))] + [HBM] * len(operands.arrays),
        out_specs=(whole, whole),
        scratch_shapes=[
            pltpu.VMEM((2, BLOCK, width), jnp.bfloat16),
            pltpu.VMEM((8, 2, BLOCK, width), jnp.bfloat16),
            pltpu.VMEM((6, heads, BLOCK, BLOCK), jnp.float32),
            pltpu.VMEM((heads, BLOCK, HEAD), jnp.float32),
            pltpu.VMEM((heads, BLOCK, HEAD), jnp.float32),
            pltpu.VMEM((2, BLOCK, HEAD), jnp.bfloat16),
            pltpu.VMEM((6, BLOCK, HEAD), jnp.bfloat16),
            pltpu.SemaphoreType.DMA((2,)),
            pltpu.SemaphoreType.DMA((8, 2)),
        ],
        compiler_params=ROOM,
        cost_estimate=CHEAP,
    )(plan, bounds, *operands.arrays)


def far_kernel(heads, pairs, own_views, plan_ref, *rest):
    width = heads * HEAD
    refs, rest = rest[:-10], rest[-10:]
    out_ref, raw, packed, own, scores, best, sums, qa_ref, ka_ref, sem = rest
    core = plan_ref[ODD]
    here = plan_ref[FAR_HERE] > 0

    @pl.when(here)
    def work():
        waits = []

        def load(view, target, number):
            halves = view if isinstance(view, tuple) else (view,)
            part = width // len(halves)
            for n, half in enumerate(halves):
                to = target.at[:, pl.ds(n * part, part)]
                options = copies_of(refs, half, part, to, sem.at[number, n], core)
                start_copies(options, core)
                waits.append(options[0][1])

        for i, pair in enumerate(pairs):
            for j in range(2):
                load(pair[j], raw.at[i, j], 2 * i + j)
        for i in range(2):
            for j in range(2):
                load(own_views[i][j], own.at[i, j], 10 + 2 * i + j)
        row = lax.broadcasted_iota(jnp.int32, (BLOCK, HEAD), 0)
        lane = lax.broadcasted_iota(jnp.int32, (BLOCK, HEAD), 1)
        from_right = row < plan_ref[EDGE]
        of_left = jnp.where(row >= BLOCK - plan_ref[REACH], 1.0, 0.0)
        of_right = jnp.where(from_right, 1.0, 0.0)
        lefts = jnp.where(lane == 0, 1.0, 0.0)
        rights = jnp.where(lane == 1, 1.0, 0.0)
        qa_ref[...] = ((of_left * lefts + of_right * rights) * FAR).astype(jnp.bfloat16)
        ka_ref[0] = (lefts * (1.0 - of_left) + rights * (1.0 - of_right)).astype(jnp.bfloat16)
        ka_ref[1] = (lefts * (1.0 - of_right) + rights * (1.0 - of_left)).astype(jnp.bfloat16)
        ka_ref[2] = jnp.zeros((BLOCK, HEAD), jnp.bfloat16)
        for copy in waits:
            copy().wait()
        for i in range(5):
            for h in range(heads):
                left = raw[i, 0, :, columns(h)].astype(jnp.float32)
                right = raw[i, 1, :, columns(h)].astype(jnp.float32)
                packed[i, :, columns(h)] = jnp.where(from_right, right, left).astype(jnp.bfloat16)

        def query_of(h):
            return jnp.concatenate([packed[0, :, columns(h)], qa_ref[...]], axis=1)

        def key_of(number, h):
            if number < 2:
                key = packed[1 + 2 * number, :, columns(h)]
            else:
                key = own[number - 2, 0, :, columns(h)]
            return jnp.concatenate([key, ka_ref[min(number, 2)]], axis=1)

        def value_of(number, h):
            if number < 2:
                return packed[2 + 2 * number, :, columns(h)]
            return own[number - 2, 1, :, columns(h)]

        def out(blocks):
            for h in range(heads):
                out_ref[:, columns(h)] = blocks[h].astype(jnp.bfloat16)

        blocks = [(n, True) for n in range(4)]
        softmax_mix(heads, blocks, query_of, key_of, value_of, scores, best, sums, out)


def attend_far(heads, plan, operands, pairs, own_views):
    width = heads * HEAD
    shape = (BLOCK, width)
    return pl.pallas_call(
        functools.partial(far_kernel, heads, pairs, own_views),
        out_shape=jax.ShapeDtypeStruct(shape, jnp.bfloat16),
        in_specs=[SMEM] + [HBM] * len(operands.arrays),
        out_specs=pl.BlockSpec(shape, lambda: (0,) * len(shape)),
        scratch_shapes=[
            pltpu.VMEM((5, 2, BLOCK, width), jnp.bfloat16),
            pltpu.VMEM((5, BLOCK, width), jnp.bfloat16),
            pltpu.VMEM((2, 2, BLOCK, width), jnp.bfloat16),
            pltpu.VMEM((4, heads, BLOCK, BLOCK), jnp.float32),
            pltpu.VMEM((heads, BLOCK, HEAD), jnp.float32),
            pltpu.VMEM((heads, BLOCK, HEAD), jnp.float32),
            pltpu.VMEM((BLOCK, HEAD), jnp.bfloat16),
            pltpu.VMEM((3, BLOCK, HEAD), jnp.bfloat16),
            pltpu.SemaphoreType.DMA((15, 2)),
        ],
        compiler_params=ROOM,
        cost_estimate=CHEAP,
    )(plan, *operands.arrays)


def finish_kernel(plan_ref, *refs):
    keep0, back0, keep1, back1, mine0, other0, mine1, other1, out_ref = refs
    core = plan_ref[ODD]
    row = lax.broadcasted_iota(jnp.int32, (BLOCK, HEAD), 0)
    low = jnp.where(core == 0, 0, plan_ref[GONE_HIGH])
    high = jnp.where(core == 0, plan_ref[GONE_LOW], BLOCK)
    gone = (row >= low) & (row < high)
    for half, (first, second, home) in enumerate(
        ((keep0, keep1, (mine0, mine1)), (back0, back1, (other0, other1)))
    ):
        for h in range(HALF_HEADS):
            start = (core if half == 0 else 1 - core) * HALF + h * HEAD
            to = pl.ds(pl.multiple_of(start, HEAD), HEAD)
            rest = (first[:, columns(h)], second[:, columns(h)])
            for step in range(2):
                block = jnp.where(
                    gone, home[step][:, columns(h)].astype(jnp.float32), rest[step].astype(jnp.float32)
                )
                out_ref[step, :, to] = block.astype(jnp.bfloat16)


def finish(plan, *arrays):
    return pl.pallas_call(
        finish_kernel,
        out_shape=jax.ShapeDtypeStruct((2, BLOCK, HEADS * HEAD), jnp.bfloat16),
        in_specs=[SMEM] + [VMEM] * len(arrays),
        out_specs=VMEM,
        compiler_params=ROOM,
        cost_estimate=CHEAP,
    )(plan, *arrays)


def shards(projections, stale_cache, positions, clip_lengths, q_gain, k_gain):
    peers = lax.axis_size("patch")
    chips = peers // 2
    device = lax.axis_index("patch").astype(jnp.int32)
    core = device % 2
    odd = core == 1

    def send(x, pairs):
        return lax.ppermute(x, "patch", pairs)

    def straight(by):
        return [(2 * c + t, 2 * (c + by) + t) for c in range(chips) for t in range(2) if 0 <= c + by < chips]

    def spread(to_right, to_other):
        pairs = []
        for c in range(chips):
            for t in range(2):
                there = c + (1 if t == to_right else -1)
                if 0 <= there < chips:
                    pairs.append((2 * c + t, 2 * there + (t ^ to_other)))
        return pairs

    def homeward(crossed):
        pairs = []
        for c in range(chips):
            for t in range(2):
                down = (t == 1) != crossed
                there = c + (-1 if down else 1)
                if 0 <= there < chips:
                    pairs.append((2 * c + t, 2 * there + (1 if down else 0)))
        return pairs

    swap_pairs = [(i, i ^ 1) for i in range(peers)]
    right, left = straight(1), straight(-1)

    def after(value, *others):
        return lax.optimization_barrier((value,) + others)[0]

    core_word = core[None]
    wide = (2, BLOCK, HALF)

    stale_mine, stale_other, raw_other = slices(core_word, stale_cache, projections)
    first_a = send(stale_mine, spread(1, 0))
    first_b = send(stale_other, spread(1, 1))
    raw_peer = send(raw_other, swap_pairs)
    peer_positions = send(positions, swap_pairs)
    plan, bounds = make_plan(device[None], clip_lengths)

    class Views(Operands):
        def stale(self, which, i, column=0):
            return self.pick(which, self.view(stale_mine, i, column=column), self.view(raw_peer, i, column=column))

        def value(self, which, step, column=0):
            mine = self.view(projections, step, 2, column=column, shared=True)
            return self.pick(which, mine, self.view(raw_peer, 2 + step, column=column))

        def key(self, which, step, column=0):
            mine = self.view(kq, 2 * step, column=column)
            return self.pick(which, mine, self.view(kq_peer, 2 * step, column=column))

        def query(self, which, step, column=0):
            mine = self.view(kq, 2 * step + 1, column=column)
            return self.pick(which, mine, self.view(kq_peer, 2 * step + 1, column=column))

        def near(self, which, i):
            a, b = self.view(first_a, i), self.view(first_b, i)
            return [(1 - which,) + a[0][1:], (which,) + b[0][1:]]

        def pick(self, which, mine, peer):
            return self.high(mine, peer) if which else self.low(mine, peer)

        def both(self, array, column=0):
            return self.view(array, 0, column=column), self.view(array, 1, column=column)

    ops = Views()
    rows = []
    for out, flag in ((0, FAR_ABOVE), (1, FAR_BELOW)):
        for i in range(2):
            rows.append((out, i, HALF, [(flag, 0, ops.stale(out, i)), (flag, 1, ops.value(1 - out, i))]))
    message_l, message_r = messages(plan, ops, (wide, wide), rows)
    second_l = send(message_l, right)
    second_r = send(message_r, left)

    tables = jnp.stack([rope_tables(positions), rope_tables(peer_positions)])
    gains = jnp.stack([q_gain, k_gain, partners(q_gain), partners(k_gain)])
    kq, kq_peer = prepare(after(core_word, message_l), projections, raw_peer, tables, gains, partner_table())

    ops = Views()
    rows = []
    for out, flag in ((0, FAR_ABOVE), (1, FAR_BELOW)):
        near = 1 - out
        rows.append((out, 0, HALF, [(None, 0, ops.key(near, 0))]))
        rows.append((out, 1, HALF, [(flag, 0, ops.value(near, 0)), (flag, 1, ops.query(near, 0))]))
        rows.append((2 + out, 0, HALF, [(flag, 0, ops.key(out, 0)), (flag, 1, ops.query(near, 1))]))
        rows.append((2 + out, 1, HALF, [(flag, 0, ops.value(out, 0)), (flag, 1, ops.key(near, 1))]))
    third_out_l, third_out_r, fourth_out_l, fourth_out_r = messages(
        plan, ops, (wide,) * 4, rows
    )
    third_l = send(third_out_l, right)
    third_r = send(third_out_r, left)

    fourth_l = send(after(fourth_out_l, first_a, first_b), right)
    fourth_r = send(after(fourth_out_r, first_a, first_b), left)

    second_l, second_r = lax.optimization_barrier((second_l, second_r))
    ops = Views()
    keep0, give0 = attend_own(
        HALF_HEADS, after(plan, third_out_l), bounds, ops,
        [ops.query(0, 0), ops.query(1, 0)],
        [
            (ops.key(0, 0), ops.value(0, 0)),
            (ops.key(1, 0), ops.value(1, 0)),
            (ops.stale(0, 0), ops.stale(0, 1)),
            (ops.stale(1, 0), ops.stale(1, 1)),
            (ops.near(0, 0), ops.near(0, 1)),
            ops.both(second_l),
            (ops.near(1, 0), ops.near(1, 1)),
            ops.both(second_r),
        ],
    )
    back0 = send(give0, swap_pairs)

    def far_step(step, plan, query_key):
        ops = Views()
        if step == 0:
            old = [(ops.near(0, i), ops.near(1, i)) for i in range(2)]
            own = [(ops.stale(i, 0), ops.stale(i, 1)) for i in range(2)]
        else:
            old = [
                (ops.view(third_l, 0), ops.view(third_r, 0)),
                (ops.view(second_l, 0), ops.view(second_r, 0)),
            ]
            own = [(ops.key(i, 0), ops.value(i, 0)) for i in range(2)]
        pairs = [tuple(query_key(ops, side, i) for side in range(2)) for i in range(2)]
        pairs += [(ops.view(second_l, step), ops.view(second_r, step))] + old
        return attend_far(HALF_HEADS, plan, ops, pairs, own)

    far0 = far_step(0, after(plan, give0), lambda ops, side, i: ops.view((third_l, third_r)[side], 1 - i))
    home0 = send(far0, homeward(False)), send(far0, homeward(True))
    far1 = far_step(
        1, after(plan, back0), lambda ops, side, i: ops.view((fourth_l, fourth_r)[side], i)
    )
    home1 = send(far1, homeward(False)), send(far1, homeward(True))
    ops = Views()
    keep1, give1 = attend_own(
        HALF_HEADS, after(plan, far1, *home0), bounds, ops,
        [ops.query(0, 1), ops.query(1, 1)],
        [
            (ops.key(0, 1), ops.value(0, 1)),
            (ops.key(1, 1), ops.value(1, 1)),
            (ops.key(0, 0), ops.value(0, 0)),
            (ops.key(1, 0), ops.value(1, 0)),
            ops.both(third_l),
            ops.both(fourth_l),
            ops.both(third_r),
            ops.both(fourth_r),
        ],
        {4: ops.view(second_l, 0), 6: ops.view(second_r, 0)},
    )
    back1 = send(give1, swap_pairs)
    return finish(plan, keep0, back0, keep1, back1, *home0, *home1)


def solution(mesh):
    return jax.shard_map(
        shards,
        mesh=mesh,
        in_specs=(
            P(None, None, ("batch", "patch"), None),
            P(None, ("batch", "patch"), None),
            P(None, ("batch", "patch")),
            P("batch"),
            P(),
            P(),
        ),
        out_specs=P(None, ("batch", "patch"), None),
        check_vma=False,
    )
```

```python
import functools

import jax
import jax.numpy as jnp
import numpy as np
from jax import lax
from jax.experimental import pallas as pl
from jax.experimental.pallas import tpu as pltpu
from jax.sharding import PartitionSpec as P

HEADS = 12
HEAD = 128
BLOCK = 256
HALF_HEADS = HEADS // 2
HALF = HALF_HEADS * HEAD
THETA = 256.0
SECTIONS = (16, 56, 56)
FAR = -(2.0**100)
LOG2E = 1.4426950408889634
SCORE_SCALE = LOG2E / float(HEAD) ** 0.5
FIRST_HALVES = ((0, 8), (16, 28), (72, 28))


def rope_tables(positions):
    section, frequency = [], []
    for number, width in enumerate(SECTIONS):
        halfway = width // 2
        exponent = -2.0 * jnp.arange(halfway, dtype=jnp.float32) / width
        one = jnp.power(jnp.float32(THETA), exponent)
        frequency += [one, one]
        section += [number] * width
    frequency = jnp.concatenate(frequency)[None, :]
    section = jnp.asarray(np.array(section, np.int32))[None, :]
    place = positions.astype(jnp.float32)[:, :, None]
    angles = jnp.where(section == 0, place[0], jnp.where(section == 1, place[1], place[2])) * frequency
    return jnp.stack([jnp.cos(angles), jnp.sin(angles)])


def partner_table():
    table = np.zeros((HEAD, HEAD), np.float32)
    for first, count in FIRST_HALVES:
        for e in range(first, first + count):
            table[e + count, e] = -1.0
            table[e, e + count] = 1.0
    return jnp.asarray(table, jnp.bfloat16)


def partners(gain):
    gain = gain.reshape(HEADS, HEAD)
    pieces = []
    for first, count in FIRST_HALVES:
        pieces += [gain[:, first + count : first + 2 * count], gain[:, first : first + count]]
    return jnp.concatenate(pieces, axis=1).reshape(HEADS * HEAD)


HBM = pl.BlockSpec(memory_space=pltpu.HBM)
VMEM = pl.BlockSpec(memory_space=pltpu.VMEM)
SMEM = pl.BlockSpec(memory_space=pltpu.SMEM)
CHEAP = pl.CostEstimate(flops=1, bytes_accessed=1, transcendentals=0)
ROOM = pltpu.CompilerParams(vmem_limit_bytes=63 * 2**20)


def columns(h):
    return slice(h * HEAD, (h + 1) * HEAD)


def when(condition, body):
    if condition is True:
        body()
    else:
        pl.when(condition)(body)


ODD, FAR_BELOW, FAR_HERE, FAR_ABOVE, EDGE, REACH, GONE_LOW, GONE_HIGH, FIRST = range(9)
USE = 9
WORDS = 21
BLOCK_STEPS = (0, 1, -1, -2, 2, 3)


def plan_kernel(device_ref, lengths_ref, plan_ref, bounds_ref):
    device = device_ref[0]
    base = (device // 2) * (2 * BLOCK)
    span = 2 * BLOCK
    clips = lengths_ref.shape[0]
    zero = jnp.int32(0)
    lane = lax.broadcasted_iota(jnp.int32, (8, HEAD), 1)
    low_bound = jnp.full((8, HEAD), 2**30, jnp.int32)
    high_bound = jnp.zeros((8, HEAD), jnp.int32)
    far = [zero, zero, zero]
    edge, reach, gone_low, gone_high = zero, zero, zero, jnp.int32(BLOCK)
    use = [[zero] * 6, [zero] * 6]
    start = zero
    for clip in range(clips):
        end = start + lengths_ref[clip]
        low_bound = jnp.where(lane == clip, start, low_bound)
        high_bound = jnp.where(lane == clip, end, high_bound)
        inside = []
        for step in BLOCK_STEPS:
            at = base + step * BLOCK
            inside.append(jnp.where((start < at + BLOCK) & (end > at), 1, 0))
        for side in range(2):
            use[side] = [u | (inside[side] & i) for u, i in zip(use[side], inside)]
        covers = []
        for by in (-1, 0, 1):
            at = base + by * span
            covers.append(jnp.where((start < at) & (end > at + span), 1, 0))
        far = [f | c for f, c in zip(far, covers)]
        edge = jnp.where(covers[1] > 0, end - base - span, edge)
        reach = jnp.where(covers[1] > 0, base - start, reach)
        gone_low = jnp.where(covers[0] > 0, end - base, gone_low)
        gone_high = jnp.where(covers[2] > 0, start - base - BLOCK, gone_high)
        start = end
    words = [device % 2] + far + [edge, reach, gone_low, gone_high, base]
    for side in range(2):
        words += use[side][:2]
        words += [u & (1 - far[0]) for u in use[side][2:4]]
        words += [u & (1 - far[2]) for u in use[side][4:6]]
    for place, word in enumerate(words):
        plan_ref[place] = word
    bounds_ref[0] = low_bound
    bounds_ref[1] = high_bound


def make_plan(device, clip_lengths):
    return pl.pallas_call(
        plan_kernel,
        out_shape=(
            jax.ShapeDtypeStruct((WORDS,), jnp.int32),
            jax.ShapeDtypeStruct((2, 8, HEAD), jnp.int32),
        ),
        in_specs=[SMEM, SMEM],
        out_specs=(SMEM, pl.BlockSpec(memory_space=pltpu.VMEM)),
        compiler_params=ROOM,
        cost_estimate=CHEAP,
    )(device, clip_lengths)


def one_hot(bounds_ref, first):
    token = first + lax.broadcasted_iota(jnp.int32, (BLOCK, HEAD), 0)
    return (token >= bounds_ref[0, :1, :]) & (token < bounds_ref[1, :1, :])


class Operands:
    def __init__(self):
        self.arrays = []

    def place(self, array):
        for at, held in enumerate(self.arrays):
            if held is array:
                return at
        self.arrays.append(array)
        return len(self.arrays) - 1

    def view(self, array, *lead, column=0, shared=False):
        return [(True, self.place(array), lead, column, shared)]

    def low(self, mine, peer):
        return [(0,) + mine[0][1:], (1,) + peer[0][1:]]

    def high(self, mine, peer):
        return [(1,) + mine[0][1:], (0,) + peer[0][1:]]


def copies_of(refs, view, width, target, sem, core):
    result = []
    for wanted, place, lead, column, shared in view:
        if shared:
            column = pl.multiple_of(core * HALF + column, HEAD)
        source = refs[place].at[lead + (slice(None), pl.ds(column, width))]
        result.append((wanted, functools.partial(pltpu.make_async_copy, source, target, sem)))
    return result


def start_copies(options, core, condition=True):
    for wanted, copy in options:
        parts = []
        if wanted is not True:
            parts.append(core == wanted)
        if condition is not True:
            parts.append(condition)
        begin = lambda copy=copy: copy().start()
        if not parts:
            begin()
        else:
            pl.when(functools.reduce(jnp.logical_and, parts))(begin)


def slice_kernel(core_ref, stale_ref, raw_ref, mine_ref, other_ref, swap_ref, buf, in_sem, out_sem):
    here = pl.multiple_of(core_ref[0] * HALF, HEAD)
    there = pl.multiple_of((1 - core_ref[0]) * HALF, HEAD)
    rows = []
    for i in range(2):
        rows.append((stale_ref.at[i, :, pl.ds(here, HALF)], [mine_ref.at[i]]))
        rows.append((stale_ref.at[i, :, pl.ds(there, HALF)], [other_ref.at[i], swap_ref.at[i]]))
    for i in range(2):
        rows.append((raw_ref.at[i, 2, :, pl.ds(there, HALF)], [swap_ref.at[2 + i]]))
    for i in range(2):
        for kind in range(2):
            rows.append((raw_ref.at[i, kind, :, pl.ds(there, HALF)], [swap_ref.at[4 + 2 * i + kind]]))
    through(rows, buf, in_sem, out_sem)


def through(rows, buf, in_sem, out_sem):
    loads = [
        pltpu.make_async_copy(source, buf.at[n], in_sem.at[n]) for n, (source, _) in enumerate(rows)
    ]
    for load in loads:
        load.start()
    stores = []
    for n, (_, targets) in enumerate(rows):
        loads[n].wait()
        for target in targets:
            store = pltpu.make_async_copy(buf.at[n], target, out_sem.at[len(stores)])
            store.start()
            stores.append(store)
    for store in stores:
        store.wait()


def slices(core, stale_cache, projections):
    def shape(n):
        return jax.ShapeDtypeStruct((n, BLOCK, HALF), jnp.bfloat16)

    return pl.pallas_call(
        slice_kernel,
        out_shape=(shape(2), shape(2), shape(8)),
        in_specs=[SMEM, HBM, HBM],
        out_specs=(HBM, HBM, HBM),
        scratch_shapes=[
            pltpu.VMEM((10, BLOCK, HALF), jnp.bfloat16),
            pltpu.SemaphoreType.DMA((10,)),
            pltpu.SemaphoreType.DMA((12,)),
        ],
        compiler_params=ROOM,
        cost_estimate=CHEAP,
    )(core, stale_cache, projections)


def prepare_kernel(core_ref, raw_ref, peer_ref, tables_ref, gains_ref, partner_ref, *outs):
    average = jnp.full((2 * HEAD, HEAD), 1.0 / HEAD, jnp.bfloat16)
    for part, raw in enumerate((raw_ref, peer_ref)):
        cosines, sines = tables_ref[part, 0], tables_ref[part, 1]
        for head in range(HALF_HEADS):
            for kind in range(2):
                row = raw[0, kind, :, columns(head)] if part == 0 else raw[kind, :, columns(head)]
                x = row.astype(jnp.float32)
                square = x * x
                high = square.astype(jnp.bfloat16)
                low = (square - high.astype(jnp.float32)).astype(jnp.bfloat16)
                mean = jnp.dot(
                    jnp.concatenate([high, low], axis=1), average, preferred_element_type=jnp.float32
                )
                other = jnp.dot(row, partner_ref[...], preferred_element_type=jnp.float32)
                inverse = lax.rsqrt(mean + 1e-06)
                normed = x * inverse * gains_ref[kind : kind + 1, columns(head)]
                turned = other * inverse * gains_ref[2 + kind : 3 + kind, columns(head)]
                rotated = normed * cosines + turned * sines
                outs[part][1 - kind, :, columns(head)] = rotated.astype(jnp.bfloat16)


def prepare(core, projections, raw_peer, tables, gains, partner):
    shape = jax.ShapeDtypeStruct((4, BLOCK, HALF), jnp.bfloat16)
    out = pl.BlockSpec((2, BLOCK, HALF), lambda i, core: (i, 0, 0))
    return pl.pallas_call(
        prepare_kernel,
        grid_spec=pltpu.PrefetchScalarGridSpec(
            num_scalar_prefetch=1,
            grid=(2,),
            in_specs=[
                pl.BlockSpec((1, 2, BLOCK, HALF), lambda i, core: (i, 0, 0, core[0])),
                pl.BlockSpec((2, BLOCK, HALF), lambda i, core: (2 + i, 0, 0)),
                pl.BlockSpec((2, 2, BLOCK, HEAD), lambda i, core: (0, 0, 0, 0)),
                pl.BlockSpec((4, HALF), lambda i, core: (0, core[0])),
                pl.BlockSpec((HEAD, HEAD), lambda i, core: (0, 0)),
            ],
            out_specs=(out, out),
        ),
        out_shape=(shape, shape),
        compiler_params=ROOM,
        cost_estimate=CHEAP,
    )(core, projections, raw_peer, tables, gains, partner)


def message_kernel(rows, count, plan_ref, *rest):
    refs, outs, (buf, in_sem, out_sem) = rest[:count], rest[count:-3], rest[-3:]
    core = plan_ref[ODD]
    loads, stores = [], []
    for number, (out, lead, width, choices) in enumerate(rows):
        target = buf.at[number, :, pl.ds(0, width)]
        for flag, value, view in choices:
            options = copies_of(refs, view, width, target, in_sem.at[number], core)
            condition = True if flag is None else plan_ref[flag] == value
            start_copies(options, core, condition)
        loads.append(options[0][1])
        stores.append(pltpu.make_async_copy(target, outs[out].at[lead], out_sem.at[number]))
    for load, store in zip(loads, stores):
        load().wait()
        store.start()
    for store in stores:
        store.wait()


def messages(plan, operands, outs, rows):
    return pl.pallas_call(
        functools.partial(message_kernel, rows, len(operands.arrays)),
        out_shape=tuple(jax.ShapeDtypeStruct(o, jnp.bfloat16) for o in outs),
        in_specs=[SMEM] + [HBM] * len(operands.arrays),
        out_specs=tuple(HBM for _ in outs),
        scratch_shapes=[
            pltpu.VMEM((len(rows), BLOCK, HALF), jnp.bfloat16),
            pltpu.SemaphoreType.DMA((len(rows),)),
            pltpu.SemaphoreType.DMA((len(rows),)),
        ],
        compiler_params=ROOM,
        cost_estimate=CHEAP,
    )(plan, *operands.arrays)


def softmax_mix(heads, blocks, query_of, key_of, value_of, scores, best, sums, out, ready=None):
    heads = range(heads)
    first = blocks[0][0]
    for number, condition in blocks:

        def score(number=number):
            if ready is not None:
                ready(number)
            for h in heads:
                s = lax.dot_general(
                    query_of(h),
                    key_of(number, h),
                    (((1,), (1,)), ((), ())),
                    preferred_element_type=jnp.float32,
                )
                scores[number, h] = s
                m = jnp.maximum(s[:, :HEAD], s[:, HEAD:])
                best[h] = m if number == first else jnp.maximum(best[h], m)

        when(condition, score)
    for h in heads:
        top = jnp.max(best[h], axis=1, keepdims=True) * SCORE_SCALE
        best[h] = jnp.broadcast_to(top, (BLOCK, HEAD))
    for number, condition in blocks:

        def lift(number=number):
            for h in heads:
                top = best[h]
                low = jnp.exp2(scores[number, h, :, :HEAD] * SCORE_SCALE - top)
                high = jnp.exp2(scores[number, h, :, HEAD:] * SCORE_SCALE - top)
                scores[number, h, :, :HEAD] = low
                scores[number, h, :, HEAD:] = high
                sums[h] = low + high if number == first else sums[h] + (low + high)

        when(condition, lift)
    for h in heads:
        inverse = 1.0 / jnp.sum(sums[h], axis=1, keepdims=True)
        sums[h] = jnp.broadcast_to(inverse, (BLOCK, HEAD))
    for number, condition in blocks:

        def mix(number=number):
            for h in heads:
                inverse = sums[h]
                low = (scores[number, h, :, :HEAD] * inverse).astype(jnp.bfloat16)
                high = (scores[number, h, :, HEAD:] * inverse).astype(jnp.bfloat16)
                part = jnp.dot(
                    jnp.concatenate([low, high], axis=1),
                    value_of(number, h),
                    preferred_element_type=jnp.float32,
                )
                best[h] = part if number == first else best[h] + part

        when(condition, mix)
    out(best)


def own_kernel(heads, queries, views, switched, plan_ref, bounds_ref, *rest):
    width = heads * HEAD
    refs, rest = rest[:-11], rest[-11:]
    outs, rest = rest[:2], rest[2:]
    q_buf, kv_buf, scores, best, sums, qa_ref, ka_ref, q_sem, kv_sem = rest
    core = plan_ref[ODD]

    def use(side, number):
        return plan_ref[USE + 6 * side + number] > 0

    def needed(number):
        return plan_ref[USE + number] + plan_ref[USE + 6 + number] > 0

    def options(slot, i, view):
        return copies_of(refs, view, width, kv_buf.at[slot, i], kv_sem.at[slot, i], core)

    def fetch(slot, condition=True, which=(0, 1)):
        for i in which:
            start_copies(options(slot, i, views[slot][i]), core, condition)

    def arrived(slot):
        for i in range(2):
            options(slot, i, views[slot][i])[0][1]().wait()

    query_options = [
        copies_of(refs, queries[side], width, q_buf.at[side], q_sem.at[side], core)
        for side in range(2)
    ]
    start_copies(query_options[0], core)
    fetch(0)
    fetch(3, use(0, 1))
    for number in range(2, 6):
        slot = number + 2
        if switched and slot in switched:
            far = plan_ref[FAR_HERE] > 0
            fetch(slot, needed(number), (0,))
            fetch(slot, jnp.logical_and(needed(number), jnp.logical_not(far)), (1,))
            start_copies(
                options(slot, 1, switched[slot]), core, jnp.logical_and(needed(number), far)
            )
        else:
            fetch(slot, needed(number))
    start_copies(query_options[1], core)
    fetch(1)
    fetch(2, use(1, 0))

    first = plan_ref[FIRST]
    for number, step in enumerate(BLOCK_STEPS):

        def mask(number=number, step=step):
            inside = one_hot(bounds_ref, first + step * BLOCK)
            ka_ref[number] = jnp.where(inside, 0.0, 1.0).astype(jnp.bfloat16)
            if number < 2:
                qa_ref[number] = jnp.where(inside, FAR, 0.0).astype(jnp.bfloat16)

        when(True if number < 2 else needed(number), mask)

    for side in range(2):
        query_options[side][0][1]().wait()

        def slot_of(number, side=side):
            if number >= 2:
                return number + 2
            return number if number == side else number + 2

        def ready(number, side=side):
            if side == 1 and number >= 2:
                pl.when(jnp.logical_not(use(0, number)))(lambda: arrived(slot_of(number)))
            else:
                arrived(slot_of(number))

        def query_of(h, side=side):
            return jnp.concatenate([q_buf[side, :, columns(h)], qa_ref[side]], axis=1)

        def key_of(number, h):
            return jnp.concatenate([kv_buf[slot_of(number), 0, :, columns(h)], ka_ref[number]], axis=1)

        def value_of(number, h):
            return kv_buf[slot_of(number), 1, :, columns(h)]

        def out(blocks, side=side):
            for place in range(2):

                @pl.when(core == (side + place) % 2)
                def store():
                    for h in range(heads):
                        outs[place][:, columns(h)] = blocks[h].astype(jnp.bfloat16)

        blocks = [(side, True)] + [(n, use(side, n)) for n in [1 - side] + list(range(2, 6))]
        softmax_mix(heads, blocks, query_of, key_of, value_of, scores, best, sums, out, ready)


def attend_own(heads, plan, bounds, operands, queries, views, switched=None):
    width = heads * HEAD
    shape = jax.ShapeDtypeStruct((BLOCK, width), jnp.bfloat16)
    whole = pl.BlockSpec((BLOCK, width), lambda i: (0, 0))
    return pl.pallas_call(
        functools.partial(own_kernel, heads, queries, views, switched),
        grid=(1,),
        out_shape=(shape, shape),
        in_specs=[SMEM, pl.BlockSpec((2, 8, HEAD), lambda i: (0, 0, 0))] + [HBM] * len(operands.arrays),
        out_specs=(whole, whole),
        scratch_shapes=[
            pltpu.VMEM((2, BLOCK, width), jnp.bfloat16),
            pltpu.VMEM((8, 2, BLOCK, width), jnp.bfloat16),
            pltpu.VMEM((6, heads, BLOCK, BLOCK), jnp.float32),
            pltpu.VMEM((heads, BLOCK, HEAD), jnp.float32),
            pltpu.VMEM((heads, BLOCK, HEAD), jnp.float32),
            pltpu.VMEM((2, BLOCK, HEAD), jnp.bfloat16),
            pltpu.VMEM((6, BLOCK, HEAD), jnp.bfloat16),
            pltpu.SemaphoreType.DMA((2,)),
            pltpu.SemaphoreType.DMA((8, 2)),
        ],
        compiler_params=ROOM,
        cost_estimate=CHEAP,
    )(plan, bounds, *operands.arrays)


def far_kernel(heads, pairs, own_views, plan_ref, *rest):
    width = heads * HEAD
    refs, rest = rest[:-10], rest[-10:]
    out_ref, raw, packed, own, scores, best, sums, qa_ref, ka_ref, sem = rest
    core = plan_ref[ODD]
    here = plan_ref[FAR_HERE] > 0

    @pl.when(here)
    def work():
        waits = []

        def load(view, target, number):
            halves = view if isinstance(view, tuple) else (view,)
            part = width // len(halves)
            for n, half in enumerate(halves):
                to = target.at[:, pl.ds(n * part, part)]
                options = copies_of(refs, half, part, to, sem.at[number, n], core)
                start_copies(options, core)
                waits.append(options[0][1])

        for i, pair in enumerate(pairs):
            for j in range(2):
                load(pair[j], raw.at[i, j], 2 * i + j)
        for i in range(2):
            for j in range(2):
                load(own_views[i][j], own.at[i, j], 10 + 2 * i + j)
        row = lax.broadcasted_iota(jnp.int32, (BLOCK, HEAD), 0)
        lane = lax.broadcasted_iota(jnp.int32, (BLOCK, HEAD), 1)
        from_right = row < plan_ref[EDGE]
        of_left = jnp.where(row >= BLOCK - plan_ref[REACH], 1.0, 0.0)
        of_right = jnp.where(from_right, 1.0, 0.0)
        lefts = jnp.where(lane == 0, 1.0, 0.0)
        rights = jnp.where(lane == 1, 1.0, 0.0)
        qa_ref[...] = ((of_left * lefts + of_right * rights) * FAR).astype(jnp.bfloat16)
        ka_ref[0] = (lefts * (1.0 - of_left) + rights * (1.0 - of_right)).astype(jnp.bfloat16)
        ka_ref[1] = (lefts * (1.0 - of_right) + rights * (1.0 - of_left)).astype(jnp.bfloat16)
        ka_ref[2] = jnp.zeros((BLOCK, HEAD), jnp.bfloat16)
        for copy in waits:
            copy().wait()
        for i in range(5):
            for h in range(heads):
                left = raw[i, 0, :, columns(h)].astype(jnp.float32)
                right = raw[i, 1, :, columns(h)].astype(jnp.float32)
                packed[i, :, columns(h)] = jnp.where(from_right, right, left).astype(jnp.bfloat16)

        def query_of(h):
            return jnp.concatenate([packed[0, :, columns(h)], qa_ref[...]], axis=1)

        def key_of(number, h):
            if number < 2:
                key = packed[1 + 2 * number, :, columns(h)]
            else:
                key = own[number - 2, 0, :, columns(h)]
            return jnp.concatenate([key, ka_ref[min(number, 2)]], axis=1)

        def value_of(number, h):
            if number < 2:
                return packed[2 + 2 * number, :, columns(h)]
            return own[number - 2, 1, :, columns(h)]

        def out(blocks):
            for h in range(heads):
                out_ref[:, columns(h)] = blocks[h].astype(jnp.bfloat16)

        blocks = [(n, True) for n in range(4)]
        softmax_mix(heads, blocks, query_of, key_of, value_of, scores, best, sums, out)


def attend_far(heads, plan, operands, pairs, own_views):
    width = heads * HEAD
    shape = (BLOCK, width)
    return pl.pallas_call(
        functools.partial(far_kernel, heads, pairs, own_views),
        out_shape=jax.ShapeDtypeStruct(shape, jnp.bfloat16),
        in_specs=[SMEM] + [HBM] * len(operands.arrays),
        out_specs=pl.BlockSpec(shape, lambda: (0,) * len(shape)),
        scratch_shapes=[
            pltpu.VMEM((5, 2, BLOCK, width), jnp.bfloat16),
            pltpu.VMEM((5, BLOCK, width), jnp.bfloat16),
            pltpu.VMEM((2, 2, BLOCK, width), jnp.bfloat16),
            pltpu.VMEM((4, heads, BLOCK, BLOCK), jnp.float32),
            pltpu.VMEM((heads, BLOCK, HEAD), jnp.float32),
            pltpu.VMEM((heads, BLOCK, HEAD), jnp.float32),
            pltpu.VMEM((BLOCK, HEAD), jnp.bfloat16),
            pltpu.VMEM((3, BLOCK, HEAD), jnp.bfloat16),
            pltpu.SemaphoreType.DMA((15, 2)),
        ],
        compiler_params=ROOM,
        cost_estimate=CHEAP,
    )(plan, *operands.arrays)


def finish_kernel(plan_ref, *refs):
    keep0, back0, keep1, back1, mine0, other0, mine1, other1, out_ref = refs
    core = plan_ref[ODD]
    row = lax.broadcasted_iota(jnp.int32, (BLOCK, HEAD), 0)
    low = jnp.where(core == 0, 0, plan_ref[GONE_HIGH])
    high = jnp.where(core == 0, plan_ref[GONE_LOW], BLOCK)
    gone = (row >= low) & (row < high)
    for half, (first, second, home) in enumerate(
        ((keep0, keep1, (mine0, mine1)), (back0, back1, (other0, other1)))
    ):
        for h in range(HALF_HEADS):
            start = (core if half == 0 else 1 - core) * HALF + h * HEAD
            to = pl.ds(pl.multiple_of(start, HEAD), HEAD)
            rest = (first[:, columns(h)], second[:, columns(h)])
            for step in range(2):
                block = jnp.where(
                    gone, home[step][:, columns(h)].astype(jnp.float32), rest[step].astype(jnp.float32)
                )
                out_ref[step, :, to] = block.astype(jnp.bfloat16)


def finish(plan, *arrays):
    return pl.pallas_call(
        finish_kernel,
        out_shape=jax.ShapeDtypeStruct((2, BLOCK, HEADS * HEAD), jnp.bfloat16),
        in_specs=[SMEM] + [VMEM] * len(arrays),
        out_specs=VMEM,
        compiler_params=ROOM,
        cost_estimate=CHEAP,
    )(plan, *arrays)


def shards(projections, stale_cache, positions, clip_lengths, q_gain, k_gain):
    peers = lax.axis_size("patch")
    chips = peers // 2
    device = lax.axis_index("patch").astype(jnp.int32)
    core = device % 2
    odd = core == 1

    def send(x, pairs):
        return lax.ppermute(x, "patch", pairs)

    def straight(by):
        return [(2 * c + t, 2 * (c + by) + t) for c in range(chips) for t in range(2) if 0 <= c + by < chips]

    def spread(to_right, to_other):
        pairs = []
        for c in range(chips):
            for t in range(2):
                there = c + (1 if t == to_right else -1)
                if 0 <= there < chips:
                    pairs.append((2 * c + t, 2 * there + (t ^ to_other)))
        return pairs

    def homeward(crossed):
        pairs = []
        for c in range(chips):
            for t in range(2):
                down = (t == 1) != crossed
                there = c + (-1 if down else 1)
                if 0 <= there < chips:
                    pairs.append((2 * c + t, 2 * there + (1 if down else 0)))
        return pairs

    swap_pairs = [(i, i ^ 1) for i in range(peers)]
    right, left = straight(1), straight(-1)

    def after(value, *others):
        return lax.optimization_barrier((value,) + others)[0]

    core_word = core[None]
    wide = (2, BLOCK, HALF)

    stale_mine, stale_other, raw_other = slices(core_word, stale_cache, projections)
    first_a = send(stale_mine, spread(1, 0))
    first_b = send(stale_other, spread(1, 1))
    raw_peer = send(raw_other, swap_pairs)
    peer_positions = send(positions, swap_pairs)
    plan, bounds = make_plan(device[None], clip_lengths)

    class Views(Operands):
        def stale(self, which, i, column=0):
            return self.pick(which, self.view(stale_mine, i, column=column), self.view(raw_peer, i, column=column))

        def value(self, which, step, column=0):
            mine = self.view(projections, step, 2, column=column, shared=True)
            return self.pick(which, mine, self.view(raw_peer, 2 + step, column=column))

        def key(self, which, step, column=0):
            mine = self.view(kq, 2 * step, column=column)
            return self.pick(which, mine, self.view(kq_peer, 2 * step, column=column))

        def query(self, which, step, column=0):
            mine = self.view(kq, 2 * step + 1, column=column)
            return self.pick(which, mine, self.view(kq_peer, 2 * step + 1, column=column))

        def near(self, which, i):
            a, b = self.view(first_a, i), self.view(first_b, i)
            return [(1 - which,) + a[0][1:], (which,) + b[0][1:]]

        def pick(self, which, mine, peer):
            return self.high(mine, peer) if which else self.low(mine, peer)

        def both(self, array, column=0):
            return self.view(array, 0, column=column), self.view(array, 1, column=column)

    ops = Views()
    rows = []
    for out, flag in ((0, FAR_ABOVE), (1, FAR_BELOW)):
        for i in range(2):
            rows.append((out, i, HALF, [(flag, 0, ops.stale(out, i)), (flag, 1, ops.value(1 - out, i))]))
    message_l, message_r = messages(plan, ops, (wide, wide), rows)
    second_l = send(message_l, right)
    second_r = send(message_r, left)

    tables = jnp.stack([rope_tables(positions), rope_tables(peer_positions)])
    gains = jnp.stack([q_gain, k_gain, partners(q_gain), partners(k_gain)])
    kq, kq_peer = prepare(after(core_word, message_l), projections, raw_peer, tables, gains, partner_table())

    ops = Views()
    rows = []
    for out, flag in ((0, FAR_ABOVE), (1, FAR_BELOW)):
        near = 1 - out
        rows.append((out, 0, HALF, [(None, 0, ops.key(near, 0))]))
        rows.append((out, 1, HALF, [(flag, 0, ops.value(near, 0)), (flag, 1, ops.query(near, 0))]))
        rows.append((2 + out, 0, HALF, [(flag, 0, ops.key(out, 0)), (flag, 1, ops.query(near, 1))]))
        rows.append((2 + out, 1, HALF, [(flag, 0, ops.value(out, 0)), (flag, 1, ops.key(near, 1))]))
    third_out_l, third_out_r, fourth_out_l, fourth_out_r = messages(
        plan, ops, (wide,) * 4, rows
    )
    third_l = send(third_out_l, right)
    third_r = send(third_out_r, left)

    fourth_l = send(after(fourth_out_l, first_a, first_b), right)
    fourth_r = send(after(fourth_out_r, first_a, first_b), left)

    second_l, second_r = lax.optimization_barrier((second_l, second_r))
    ops = Views()
    keep0, give0 = attend_own(
        HALF_HEADS, after(plan, third_out_l), bounds, ops,
        [ops.query(0, 0), ops.query(1, 0)],
        [
            (ops.key(0, 0), ops.value(0, 0)),
            (ops.key(1, 0), ops.value(1, 0)),
            (ops.stale(0, 0), ops.stale(0, 1)),
            (ops.stale(1, 0), ops.stale(1, 1)),
            (ops.near(0, 0), ops.near(0, 1)),
            ops.both(second_l),
            (ops.near(1, 0), ops.near(1, 1)),
            ops.both(second_r),
        ],
    )
    back0 = send(give0, swap_pairs)

    def far_step(step, plan, query_key):
        ops = Views()
        if step == 0:
            old = [(ops.near(0, i), ops.near(1, i)) for i in range(2)]
            own = [(ops.stale(i, 0), ops.stale(i, 1)) for i in range(2)]
        else:
            old = [
                (ops.view(third_l, 0), ops.view(third_r, 0)),
                (ops.view(second_l, 0), ops.view(second_r, 0)),
            ]
            own = [(ops.key(i, 0), ops.value(i, 0)) for i in range(2)]
        pairs = [tuple(query_key(ops, side, i) for side in range(2)) for i in range(2)]
        pairs += [(ops.view(second_l, step), ops.view(second_r, step))] + old
        return attend_far(HALF_HEADS, plan, ops, pairs, own)

    far0 = far_step(0, after(plan, give0), lambda ops, side, i: ops.view((third_l, third_r)[side], 1 - i))
    home0 = send(far0, homeward(False)), send(far0, homeward(True))
    far1 = far_step(
        1, after(plan, back0), lambda ops, side, i: ops.view((fourth_l, fourth_r)[side], i)
    )
    home1 = send(far1, homeward(False)), send(far1, homeward(True))
    ops = Views()
    keep1, give1 = attend_own(
        HALF_HEADS, after(plan, far1, *home0), bounds, ops,
        [ops.query(0, 1), ops.query(1, 1)],
        [
            (ops.key(0, 1), ops.value(0, 1)),
            (ops.key(1, 1), ops.value(1, 1)),
            (ops.key(0, 0), ops.value(0, 0)),
            (ops.key(1, 0), ops.value(1, 0)),
            ops.both(third_l),
            ops.both(fourth_l),
            ops.both(third_r),
            ops.both(fourth_r),
        ],
        {4: ops.view(second_l, 0), 6: ops.view(second_r, 0)},
    )
    back1 = send(give1, swap_pairs)
    return finish(plan, keep0, back0, keep1, back1, *home0, *home1)


def solution(mesh):
    return jax.shard_map(
        shards,
        mesh=mesh,
        in_specs=(
            P(None, None, ("batch", "patch"), None),
            P(None, ("batch", "patch"), None),
            P(None, ("batch", "patch")),
            P("batch"),
            P(),
            P(),
        ),
        out_specs=P(None, ("batch", "patch"), None),
        check_vma=False,
    )
```
